32 devices in a mesh: band: 16 (over z, y, core), grid: 2 (over x).
Axes of the slice: x: 2, y: 2, z: 4, core: 2. Of those that a mesh axis runs over, the one named last changes fastest.
Arguments:
- block_coeffs: float32 [128, 32768], P('band', 'grid'), may hold values from -6 to 6
- potential: float32 [96, 9216], P('grid'), may hold values from -4 to 4
- lower_edge: float32 [1], replicated, may hold values from 0.8 to 1.2
- upper_edge: float32 [1], replicated, may hold values from 4.5 to 5.5
- rotation: float32 [8, 3072, 8], P(None, 'band'), may hold values from -0.75 to 0.75
- owners: int32 [8], replicated, may hold values from 0 to 15
Outputs:
- filtered: float32 [128, 32768], P('band', 'grid')
- residents: float32 [3072, 32768], P('band', 'grid')
The draws below stay inside these ranges and needn't reach their ends.
All inputs are finite; a program needn't handle non-finite values.
Results may differ from the reference program's by a relative error of at most 0.000071.
Values sent between devices are 32-bit elements; how exact they have to be, the bound alone decides.
No kernel may reach another device: no remote copies, remote signals or barrier semaphores. Data moves between devices by JAX's collectives and lax.ppermute only.
A program may use at most 128 MiB of HBM per device.

```python
import jax
import jax.numpy as jnp
from jax import lax

NG = 96
KEEP = 32
BLK = 8
STEPS = 8
BANDS = 128
RBANDS = 3072
NPW = 32768
PLANE = 9216
N_BAND = 16


def plant(drawn, rng, low, top_value):
    spot = [jax.random.randint(jax.random.fold_in(rng, axis), (), 0, length) for axis, length in enumerate(drawn.shape)]
    main_axis = drawn.shape.index(max(drawn.shape))
    next_to = spot[:main_axis] + [(spot[main_axis] + 1) % drawn.shape[main_axis]] + spot[main_axis + 1:]
    return drawn.at[tuple(spot)].set(low).at[tuple(next_to)].set(top_value)


def shard_levels(own_key, shape, split, smallest, top_value):
    level = 1.0
    for dim, blocks in split:
        draws = jax.random.uniform(jax.random.fold_in(jax.random.fold_in(own_key, 6), dim), (blocks,), jnp.float32, smallest / len(split), top_value / len(split))
        level = level * jnp.repeat(jnp.exp(draws), shape[dim] // blocks).reshape((-1,) + (1,) * (len(shape) - 1 - dim))
    return level


def bell_draw(key, dims, spread, limit, shards=(), kind=jnp.bfloat16):
    result = jax.random.normal(key, dims, jnp.float32) * spread
    if len(shards) > 0:
        result = shard_levels(key, dims, shards, -0.22, 0.18) * result
    return jnp.clip(result, min=-limit, max=limit).astype(kind)


def setup_inputs(seed: int = 0) -> dict:
    key_of = jax.random.split(jax.random.key(seed), 7)
    return {
        "block_coeffs": bell_draw(key_of[0], (BANDS, NPW), 1.0, 6.0, ((0, 16), (1, 2)), jnp.float32),
        "potential": bell_draw(key_of[1], (NG, PLANE), 1.0, 4.0, ((0, 2),), jnp.float32),
        "lower_edge": jnp.clip(jax.random.uniform(key_of[2], (1,), jnp.float32, 0.8, 1.2), 0.8, 1.2),
        "upper_edge": jnp.clip(jax.random.uniform(key_of[3], (1,), jnp.float32, 4.5, 5.5), 4.5, 5.5),
        "rotation": bell_draw(key_of[4], (STEPS, RBANDS, BLK), (BLK * STEPS) ** -0.5, 0.75, ((1, 16),), jnp.float32),
        "owners": plant(jax.random.randint(key_of[5], (STEPS,), 0, N_BAND), jax.random.fold_in(key_of[5], 1), 0, N_BAND - 1).astype(jnp.int32),
    }


edge_energy = 1.3

def kept_frequency(kept_count, grid_points):
    ordinal = jnp.arange(kept_count, dtype=jnp.int32)
    return jnp.where(ordinal < kept_count // 2, ordinal, ordinal + (grid_points - kept_count))

def hartley_table(kept_count, grid_points):
    points = jnp.arange(grid_points, dtype=jnp.int32)
    phase_turns = points[:, None] * kept_frequency(kept_count, grid_points)[None, :] % grid_points
    angles = phase_turns.astype(jnp.float32) * (2.0 * jnp.pi / grid_points)
    return (jnp.cos(angles) + jnp.sin(angles)) / jnp.sqrt(jnp.float32(grid_points))

def signed_square(kept_count):
    ordinal = jnp.arange(kept_count, dtype=jnp.int32)
    signed = jnp.where(ordinal < kept_count // 2, ordinal, ordinal - kept_count).astype(jnp.float32)
    return signed * signed / jnp.float32((kept_count // 2) ** 2)

def kinetic_cube(kept_count):
    square = signed_square(kept_count)
    return edge_energy * (square[:, None, None] + square[None, :, None] + square[None, None, :])

def synthesize(coeffs, hartley):
    coef_cube = coeffs.reshape(coeffs.shape[0], KEEP, KEEP, KEEP)
    along_x = jnp.einsum('bqkz,nk->bqnz', coef_cube, hartley, precision=lax.Precision.HIGHEST)
    along_y = jnp.einsum('bqnz,yq->bnyz', along_x, hartley, precision=lax.Precision.HIGHEST)
    return jnp.einsum('bnyz,wz->bnyw', along_y, hartley, precision=lax.Precision.HIGHEST)

def analyse(real_field, hartley):
    along_z = jnp.einsum('bnyw,wz->bnyz', real_field, hartley, precision=lax.Precision.HIGHEST)
    along_y = jnp.einsum('bnyz,yq->bqnz', along_z, hartley, precision=lax.Precision.HIGHEST)
    along_x = jnp.einsum('bqnz,nk->bqkz', along_y, hartley, precision=lax.Precision.HIGHEST)
    return along_x.reshape(real_field.shape[0], NPW)

def reference(block_coeffs, potential, lower_edge, upper_edge, rotation, owners):
    hartley = hartley_table(KEEP, NG)
    kinetic = kinetic_cube(KEEP).reshape(1, NPW)
    potential_cube = potential.reshape(NG, NG, NG)
    center = (lower_edge[0] + upper_edge[0]) * 0.5
    half_width = (upper_edge[0] - lower_edge[0]) * 0.5

    def hamiltonian(coeffs):
        return kinetic * coeffs + analyse(potential_cube[None] * synthesize(coeffs, hartley), hartley)

    def filter_group(coeffs):
        first_term = (hamiltonian(coeffs) - center * coeffs) / half_width
        return 2.0 * (hamiltonian(first_term) - center * first_term) / half_width - coeffs
    grouped = lax.map(filter_group, block_coeffs.reshape(N_BAND, BLK, NPW))
    filtered = grouped.reshape(BANDS, NPW)
    stacked = grouped[owners]
    residents = jnp.einsum('sri,sin->rn', rotation, stacked, precision=lax.Precision.HIGHEST)
    return (filtered, residents)
```

```python
import functools

import jax
import jax.numpy as jnp
import ml_dtypes
import numpy as np
from jax import lax
from jax.experimental import pallas as pl
from jax.experimental.pallas import tpu as pltpu
from jax.sharding import PartitionSpec as P

NG = 96
KEEP = 32
EDGE_ENERGY = 1.3
NP = 64
LOW = 4
LANES = LOW * KEEP
QUAD = 4
MIB = 1024 * 1024

F32 = jnp.float32
BF16 = jnp.bfloat16


def cas(angle):
    return np.cos(angle) + np.sin(angle)


SIGNED = np.where(np.arange(KEEP) < KEEP // 2, np.arange(KEEP), np.arange(KEEP) - KEEP).astype(np.float64)
POINTS = 2.0 * np.pi * (np.arange(NP) + 0.5) / NP


def product_basis(points):
    return np.concatenate(
        [np.cos(points[:, None] * np.arange(KEEP)), np.sin(points[:, None] * np.arange(1, KEEP + 1))], axis=1
    )


PROJECT = np.linalg.solve(product_basis(POINTS).T, product_basis(2.0 * np.pi * np.arange(NG) / NG).T)
TABLE = cas(POINTS[:, None] * SIGNED[None, :]) / np.sqrt(NG)
KX_ORDER = np.arange(KEEP).reshape(KEEP // LOW, LOW).T.reshape(-1)


ROW_SYN, ROW_PROJECT, ROW_Y_ANA = 0, NP, 2 * NP
ROW_X_ANA = ROW_Y_ANA + KEEP
ROW_Z_SYN = ROW_X_ANA + KEEP
ROW_Z_ANA = ROW_Z_SYN + 3 * LANES
ROW_END = ROW_Z_ANA + 2 * LANES


def halves(table):
    high = table.astype(np.float32).astype(ml_dtypes.bfloat16)
    low = (table - high.astype(np.float64)).astype(np.float32).astype(ml_dtypes.bfloat16)
    return high, low


def left_table(table):
    high, low = halves(table)
    return np.concatenate([high, low, high], axis=1)


def split(x):
    high = x.astype(BF16)
    return high, (x - high.astype(F32)).astype(BF16)


def stack(x):
    high, low = split(x)
    return jnp.concatenate([high, high, low], axis=0)


def mm(a, b):
    return jnp.dot(a, b, preferred_element_type=F32)


def sheet(shape, *parts):
    whole = np.zeros(shape, ml_dtypes.bfloat16)
    for row, lane, part in parts:
        whole[row:row + part.shape[0], lane:lane + part.shape[1]] = part
    return jnp.asarray(whole)


def lane_transpose(parts):
    lane = lax.broadcasted_iota(jnp.int32, (1, LANES), 1)
    second = (lane // 64) == 1
    odd = (lane // 32) % 2 == 1
    a, b, c, d = parts
    p0 = jnp.where(second, pltpu.roll(c, 64, 1), a)
    p2 = jnp.where(second, c, pltpu.roll(a, 64, 1))
    p1 = jnp.where(second, pltpu.roll(d, 64, 1), b)
    p3 = jnp.where(second, d, pltpu.roll(b, 64, 1))
    r0 = jnp.where(odd, pltpu.roll(p1, 32, 1), p0)
    r1 = jnp.where(odd, p1, pltpu.roll(p0, 96, 1))
    r2 = jnp.where(odd, pltpu.roll(p3, 32, 1), p2)
    r3 = jnp.where(odd, p3, pltpu.roll(p2, 96, 1))
    return [r0, r1, r2, r3]


def pack_kernel(slices, c_ref, *rest):
    outs, scratch = rest[:slices], rest[slices]
    rows = scratch.shape[0] // 8
    each = 8 // slices
    g = lax.axis_index("grid")
    for r in range(rows):
        scratch[pl.ds(r, 8, stride=rows), :] = c_ref[:, r * LANES:(r + 1) * LANES]
    for k in range(slices):
        dest = lax.rem(g + k, slices)
        start = pl.multiple_of(dest * (each * rows), each * rows)
        outs[k][...] = scratch[pl.ds(start, each * rows), :].reshape(each, rows, LANES)


def unpack_kernel(slices, *refs):
    ins, out, scratch = refs[:slices], refs[slices], refs[slices + 1]
    rows = scratch.shape[0] // 8
    each = 8 // slices
    g = lax.axis_index("grid")
    for k in range(slices):
        source = lax.rem(g + slices - k, slices)
        start = pl.multiple_of(source * (each * rows), each * rows)
        scratch[pl.ds(start, each * rows), :] = ins[k][...].reshape(each * rows, LANES)
    for r in range(rows):
        out[:, r * LANES:(r + 1) * LANES] = scratch[pl.ds(r, 8, stride=rows), :]


def project_kernel(ways, v_ref, tables, after, out_ref, first, second):
    planes = out_ref.shape[0]
    start = 0
    if ways > 1:
        start = pl.multiple_of(lax.rem(lax.axis_index("band"), ways) * planes, planes)
    z_high, z_low = tables[:NG, :LANES], tables[:NG, LANES:2 * LANES]
    group = 16
    for y0 in range(0, NG, group):
        x = jnp.concatenate(
            [v_ref[pl.ds(start, planes), (y0 + i) * NG:(y0 + i + 1) * NG] for i in range(group)], axis=0
        )
        high, low = split(x)
        first[y0 * planes:(y0 + group) * planes, :] = mm(high, z_high) + mm(high, z_low) + mm(low, z_high)
    y_table = tables[NG:NG + NP, :3 * NG]
    for p in range(0, planes, 2):
        x = jnp.concatenate([first[pl.ds(p + i, NG, stride=planes), :] for i in range(2)], axis=1)
        res = mm(y_table, stack(x))
        for i in range(2):
            second[pl.ds(p + i, NP, stride=planes), :] = res[:, i * LANES:(i + 1) * LANES]
    left = lax.broadcasted_iota(jnp.int32, (1, LANES), 1) < NP
    for j in range(NP // 2):
        even = second[2 * j * planes:(2 * j + 1) * planes, :]
        odd = second[(2 * j + 1) * planes:(2 * j + 2) * planes, :]
        out_ref[:, j * LANES:(j + 1) * LANES] = jnp.where(left, even, odd)


def synthesis_kernel(slices, *refs):
    coeffs, tables = refs[:slices], refs[slices]
    c_all, field, z_first, x1 = refs[slices + 1:]
    g = lax.axis_index("grid")
    each, rows, _ = coeffs[0].shape
    ky_local = KEEP // slices
    kx_high = KEEP // LOW
    for k in range(slices):
        source = lax.rem(g + slices - k, slices)
        parts = [coeffs[k][b] if b < each else jnp.zeros((rows, LANES), F32) for b in range(QUAD)]
        for low, part in enumerate(lane_transpose(parts)):
            c_all[pl.ds(source * ky_local, ky_local), low * kx_high:(low + 1) * kx_high, :] = part.reshape(
                ky_local, kx_high, LANES
            )
    synthesize(c_all, tables, z_first, x1, lambda x, value: put(field, x * NP, value))


def put(ref, row, value):
    ref[row:row + value.shape[0], :] = value


def wide(ref, start, size, stride):
    return jnp.concatenate([ref[h, pl.ds(start, size, stride=stride), :] for h in range(2)], axis=1)


def synthesize(u_all, tables, z_first, x1, give):
    z_syn = tables[ROW_Z_SYN:ROW_Z_SYN + 3 * LANES, :2 * LANES]
    group = 8
    for ky in range(0, KEEP, group):
        high, low = split(u_all[ky:ky + group].reshape(group * KEEP, LANES))
        put(z_first, ky * KEEP, mm(jnp.concatenate([high, high, low], axis=1), z_syn))
    xs = tables[ROW_SYN:ROW_SYN + NP, :3 * KEEP]
    for ky in range(KEEP):
        res = mm(xs, stack(z_first[ky * KEEP:(ky + 1) * KEEP, :]))
        for h in range(2):
            x1[h, ky * NP:(ky + 1) * NP, :] = res[:, h * LANES:(h + 1) * LANES]
    ys = tables[ROW_SYN:ROW_SYN + NP, LANES:LANES + 3 * KEEP]
    for x in range(NP):
        give(x, mm(ys, stack(wide(x1, x, KEEP, NP))))


def filter_kernel(slices, ways, *refs):
    c_all, field = refs[:2]
    pieces = refs[2:2 + slices * ways]
    refs = refs[2 + slices * ways:]
    lower, upper, tables = refs[:3]
    outs, spread = refs[3:3 + slices], refs[3 + slices]
    planes_all, vt, u_all, z_first, x1, y2, packed = refs[4 + slices:]
    g = lax.axis_index("grid")
    core = lax.rem(lax.axis_index("band"), ways)
    each, rows, _ = outs[0].shape
    kx_high = KEEP // LOW
    planes = pieces[0].shape[0]
    slot = planes_all.shape[0] // (slices * ways)
    if slot != planes:
        planes_all[...] = jnp.zeros_like(planes_all)

    for k in range(slices):
        source = lax.rem(g + slices - k, slices)
        for w in range(ways):
            half = lax.rem(core + w, ways)
            start = pl.multiple_of((source * ways + half) * slot, slot)
            planes_all[pl.ds(start, planes), :] = pieces[k * ways + w][...]
    x_table = tables[ROW_PROJECT:ROW_PROJECT + NP, :3 * planes_all.shape[0]]
    left = lax.broadcasted_iota(jnp.int32, (1, LANES), 1) < NP
    width = 512
    for c0 in range(0, NP * NP, width):
        res = mm(x_table, stack(planes_all[:, c0:c0 + width]))
        for j in range(width // LANES):
            v = res[:, j * LANES:(j + 1) * LANES]
            turned = pltpu.roll(v, NP, 1)
            y = 2 * (c0 // LANES + j)
            vt[pl.ds(y, NP, stride=NP), :] = jnp.where(left, v, turned)
            vt[pl.ds(y + 1, NP, stride=NP), :] = jnp.where(left, turned, v)

    low_edge = jnp.full((1, LANES), lower[0], F32)
    high_edge = jnp.full((1, LANES), upper[0], F32)
    center = (low_edge + high_edge) * 0.5
    half_width = (high_edge - low_edge) * 0.5

    row = lax.broadcasted_iota(jnp.int32, (KEEP, LANES), 0)
    lane = lax.broadcasted_iota(jnp.int32, (KEEP, LANES), 1)
    kx = row % kx_high * LOW + row // kx_high
    kz = lane % KEEP
    signed = [jnp.where(k < KEEP // 2, k, k - KEEP).astype(F32) for k in (kx, kz)]
    square = signed[0] * signed[0] + signed[1] * signed[1]

    z_ana = tables[ROW_Z_ANA:ROW_Z_ANA + 2 * LANES, :2 * LANES]
    ya = tables[ROW_Y_ANA:ROW_Y_ANA + KEEP, :3 * NP]
    xa = tables[ROW_X_ANA:ROW_X_ANA + KEEP, :3 * NP]

    def weigh(x, value):
        local = vt[x * NP:(x + 1) * NP, :]
        res = mm(ya, stack(value * jnp.concatenate([local, local], axis=1)))
        for h in range(2):
            y2[h, x * KEEP:(x + 1) * KEEP, :] = res[:, h * LANES:(h + 1) * LANES]

    def finish(u, scale, back):
        for ky in range(KEEP):
            put(z_first, ky * KEEP, mm(xa, stack(wide(y2, ky, NP, KEEP))))
        group = 8
        for ky in range(0, KEEP, group):
            high, low = split(z_first[ky * KEEP:(ky + group) * KEEP, :])
            twice = mm(high, z_ana)
            res = twice[:, :LANES] + twice[:, LANES:] + mm(low, z_ana[:, :LANES])
            for i in range(group):
                kinetic = EDGE_ENERGY * ((square + SIGNED[ky + i] ** 2) * (1.0 / (KEEP // 2) ** 2))
                now = u[ky + i]
                out = scale * (kinetic * now + res[i * KEEP:(i + 1) * KEEP, :] - center * now)
                u_all[ky + i] = out - c_all[ky + i] if back else out

    for x in range(NP):
        weigh(x, field[x * NP:(x + 1) * NP, :])
    finish(c_all, 1.0 / half_width, False)
    synthesize(u_all, tables, z_first, x1, weigh)
    finish(u_all, 2.0 / half_width, True)

    parts = [
        u_all[:, low * kx_high:(low + 1) * kx_high, :].reshape(KEEP * kx_high, LANES) for low in range(LOW)
    ]
    for b, part in enumerate(lane_transpose(parts)[:each]):
        packed[b] = part
    for k in range(slices):
        dest = lax.rem(g + k, slices)
        start = pl.multiple_of(dest * rows, rows)
        for b in range(each):
            outs[k][b] = packed[b, pl.ds(start, rows), :]
    run = spread.shape[1] // each
    groups = rows // run
    for dest in range(groups * slices):
        start = (dest % slices) * rows + (dest // slices) * run
        for b in range(each):
            spread[dest, b * run:(b + 1) * run, :] = packed[b, start:start + run, :]


def select_kernel(owners, came, out):
    steps = owners.shape[0]
    run = out.shape[1] // LANES
    block = out.shape[0] // steps
    for s in range(steps):
        for r in range(run):
            start = owners[s] * (block * run) + r
            out[s * block:(s + 1) * block, r * LANES:(r + 1) * LANES] = came[pl.ds(start, block, stride=run), :]


def rotate_kernel(moves, chips, table, *refs):
    count = sum(parts for _, _, parts in moves)
    blocks = list(refs[:count])
    out, arrived, results, in_sems, out_sems = refs[-5:]
    band = lax.axis_index("band")
    chip, core = band // 2, lax.rem(band, 2)
    position = jnp.where(lax.rem(chip, 2) == 0, chip // 2, chips - 1 - chip // 2)
    slots, _, width = results.shape
    loads = []
    for j, (_, _, parts) in enumerate(moves):
        row, now = 0, []
        for _ in range(parts):
            block = blocks.pop(0)
            size = block.shape[0]
            now.append(
                pltpu.make_async_copy(block, arrived.at[j, pl.ds(row, size)], in_sems.at[len(now) * len(moves) + j])
            )
            row += size
        loads.append(now)
    for now in loads:
        for load in now:
            load.start()
    left = table[...]
    stores = []
    for j, (offset, flip, _) in enumerate(moves):
        for load in loads[j]:
            load.wait()
        res = mm(left, stack(arrived[j]))
        if j >= slots:
            stores[j - slots].wait()
        results[j % slots] = res
        place = lax.rem(position + (chips + offset), chips)
        owner = jnp.where(place < chips // 2, 2 * place, 2 * (chips - 1 - place) + 1)
        start = pl.multiple_of((2 * owner + (core if flip == 0 else 1 - core)) * width, width)
        store = pltpu.make_async_copy(
            results.at[j % slots], out.at[:, pl.ds(start, width)], out_sems.at[j % slots]
        )
        store.start()
        stores.append(store)
    for store in stores[-slots:]:
        store.wait()


def params(mib):
    return pltpu.CompilerParams(vmem_limit_bytes=mib * MIB)


def in_vmem(count):
    return [pl.BlockSpec(memory_space=pltpu.VMEM)] * count


def body(block_coeffs, potential, lower_edge, upper_edge, rotation, owners):
    slices = lax.axis_size("grid")
    groups = lax.axis_size("band")
    block, cols = block_coeffs.shape
    rows = cols // LANES
    each = block // slices
    steps = rotation.shape[0]
    ways = 2 if potential.shape[0] % 16 == 0 else 1
    planes = potential.shape[0] // ways
    slot = -(-planes // 8) * 8

    def shift(x, k):
        return lax.ppermute(x, "grid", [(i, (i + k) % slices) for i in range(slices)])

    def shift_diagonal(x, k):
        pairs = [
            (i * slices + j, (i ^ 1) * slices + (j + k) % slices) for i in range(groups) for j in range(slices)
        ]
        return lax.ppermute(x, ("band", "grid"), pairs)

    def other_core(x):
        return lax.ppermute(x, "band", [(i, i ^ 1) for i in range(groups)])

    piece = jax.ShapeDtypeStruct((each, rows, LANES), F32)
    packed = pl.pallas_call(
        functools.partial(pack_kernel, slices),
        out_shape=[piece] * slices,
        in_specs=in_vmem(1),
        out_specs=in_vmem(slices),
        scratch_shapes=[pltpu.VMEM((block * rows, LANES), F32)],
        compiler_params=params(8),
        name="pack",
    )(block_coeffs)
    coeffs = [packed[0]] + [shift(packed[k], k) for k in range(1, slices)]

    z_high, z_low = halves(np.concatenate([PROJECT.T, PROJECT.T], axis=1))
    project_tables = sheet(
        (NG + NP, 3 * LANES), (0, 0, z_high), (0, LANES, z_low), (NG, 0, left_table(PROJECT))
    )
    projected = pl.pallas_call(
        functools.partial(project_kernel, ways),
        out_shape=jax.ShapeDtypeStruct((planes, NP * NP), F32),
        in_specs=in_vmem(2) + [pl.BlockSpec(memory_space=pl.ANY)],
        out_specs=pl.BlockSpec(memory_space=pltpu.VMEM),
        scratch_shapes=[pltpu.VMEM((NG * planes, LANES), F32), pltpu.VMEM((NP * planes, LANES), F32)],
        compiler_params=params(12),
        name="project",
    )(potential, project_tables, packed[0])
    projected, coeffs = lax.optimization_barrier((projected, coeffs))
    eye = np.eye(QUAD)
    z_high, z_low = halves(np.kron(eye, TABLE.T))
    back_high, back_low = halves(np.kron(eye, TABLE))
    slots = np.zeros((NP, NG // planes, slot))
    slots[:, :, :planes] = PROJECT.reshape(NP, NG // planes, planes)
    tables = sheet(
        (ROW_END, 3 * LANES),
        (ROW_SYN, 0, left_table(TABLE[:, KX_ORDER])),
        (ROW_SYN, LANES, left_table(TABLE)),
        (ROW_PROJECT, 0, left_table(slots.reshape(NP, -1))),
        (ROW_Y_ANA, 0, left_table(TABLE.T)),
        (ROW_X_ANA, 0, left_table(TABLE[:, KX_ORDER].T)),
        (ROW_Z_SYN, 0, np.concatenate([z_high, z_low, z_high], axis=0)),
        (ROW_Z_ANA, 0, np.concatenate([back_high, back_low], axis=1)),
    )
    cube = jax.ShapeDtypeStruct((KEEP, KEEP, LANES), F32)
    c_all, field = pl.pallas_call(
        functools.partial(synthesis_kernel, slices),
        out_shape=[cube, jax.ShapeDtypeStruct((NP * NP, 2 * LANES), F32)],
        in_specs=in_vmem(slices + 1),
        out_specs=in_vmem(2),
        scratch_shapes=[
            pltpu.VMEM((KEEP * KEEP, 2 * LANES), F32),
            pltpu.VMEM((2, KEEP * NP, LANES), F32),
        ],
        compiler_params=params(16),
        cost_estimate=pl.CostEstimate(flops=1, bytes_accessed=1, transcendentals=0),
        name="synthesis",
    )(*coeffs, tables)

    pieces = []
    for k in range(slices):
        if ways == 1:
            pieces.append(projected if k == 0 else shift(projected, k))
        elif k == 0:
            pieces += [projected, other_core(projected)]
        else:
            came, c_all, field = lax.optimization_barrier((shift_diagonal(projected, k), c_all, field))
            pieces += [other_core(came), came]

    *filtered_pieces, spread = pl.pallas_call(
        functools.partial(filter_kernel, slices, ways),
        out_shape=[piece] * slices
        + [jax.ShapeDtypeStruct((groups * slices, each * rows // groups, LANES), F32)],
        in_specs=in_vmem(2 + slices * ways) + [pl.BlockSpec(memory_space=pltpu.SMEM)] * 2 + in_vmem(1),
        out_specs=in_vmem(slices + 1),
        scratch_shapes=[
            pltpu.VMEM((NG // planes * slot, NP * NP), F32),
            pltpu.VMEM((NP * NP, LANES), F32),
            pltpu.VMEM((KEEP, KEEP, LANES), F32),
            pltpu.VMEM((KEEP * KEEP, 2 * LANES), F32),
            pltpu.VMEM((2, KEEP * NP, LANES), F32),
            pltpu.VMEM((2, KEEP * NP, LANES), F32),
            pltpu.VMEM((each, KEEP * KEEP // LOW, LANES), F32),
        ],
        compiler_params=params(28),
        name="chebyshev",
    )(c_all, field, *pieces, lower_edge, upper_edge, tables)
    arrived = [filtered_pieces[0]] + [shift(filtered_pieces[k], k) for k in range(1, slices)]
    filtered = pl.pallas_call(
        functools.partial(unpack_kernel, slices),
        out_shape=jax.ShapeDtypeStruct((block, cols), F32),
        in_specs=in_vmem(slices),
        out_specs=pl.BlockSpec(memory_space=pltpu.VMEM),
        scratch_shapes=[pltpu.VMEM((block * rows, LANES), F32)],
        compiler_params=params(8),
        cost_estimate=pl.CostEstimate(flops=1, bytes_accessed=1, transcendentals=0),
        name="unpack",
    )(*arrived)

    came = lax.all_to_all(spread, ("band", "grid"), split_axis=0, concat_axis=0, tiled=True)
    width = cols // groups
    mine = pl.pallas_call(
        select_kernel,
        out_shape=jax.ShapeDtypeStruct((steps * block, width), F32),
        in_specs=[pl.BlockSpec(memory_space=pltpu.SMEM), pl.BlockSpec(memory_space=pltpu.VMEM)],
        out_specs=pl.BlockSpec(memory_space=pltpu.VMEM),
        compiler_params=params(8),
        name="select",
    )(owners, came.reshape(-1, LANES))

    chips = groups // 2
    ring = list(range(0, chips, 2)) + list(range(1, chips, 2))[::-1]

    def pass_on(x, step):
        pairs = [
            (2 * ring[p] + c, 2 * ring[(p + step) % chips] + c) for p in range(chips) for c in range(2)
        ]
        return lax.ppermute(x, "band", pairs)

    flat = jnp.transpose(rotation, (1, 0, 2)).reshape(rotation.shape[1], steps * block)
    high, low = split(flat)
    table = jnp.concatenate([high, low, high], axis=1)
    rotated_shape = jax.ShapeDtypeStruct((rotation.shape[1], cols), F32)

    def rotate(moves, before):
        arrays = [x for _, _, parts in moves for x in parts]
        plan = tuple((offset, flip, len(parts)) for offset, flip, parts in moves)
        count = len(moves)
        return pl.pallas_call(
            functools.partial(rotate_kernel, plan, chips),
            out_shape=rotated_shape,
            in_specs=[pl.BlockSpec(memory_space=pltpu.VMEM)]
            + [pl.BlockSpec(memory_space=pl.ANY)] * (len(arrays) + len(before)),
            out_specs=pl.BlockSpec(memory_space=pl.ANY),
            scratch_shapes=[
                pltpu.VMEM((count, steps * block, width), F32),
                pltpu.VMEM((min(3, count), rotation.shape[1], width), F32),
                pltpu.SemaphoreType.DMA((2 * count,)),
                pltpu.SemaphoreType.DMA((min(3, count),)),
            ],
            input_output_aliases={len(arrays) + 1: 0} if before else {},
            compiler_params=params(12),
            cost_estimate=pl.CostEstimate(
                flops=200_000_000 * count, bytes_accessed=1_500_000 * count, transcendentals=0
            ),
            name="rotate",
        )(table, *arrays, *before)

    half = chips // 2
    right = left = mine
    ready, later = [(0, 0, [mine]), (0, 1, [other_core(mine)])], []
    rotated = []
    for k in range(1, half):
        right, left = pass_on(right, 1), pass_on(left, -1)
        if k == half - 1:
            filtered, right, left, early = lax.optimization_barrier((filtered, right, left, rotate(ready, rotated)))
            ready, rotated = [], [early]
        ready += [(-k, 0, [right]), (k, 0, [left])] + later
        later = [(-k, 1, [other_core(right)]), (k, 1, [other_core(left)])]
    last = [
        pass_on(lax.slice_in_dim(right, 0, steps * block // 2, axis=0), 1),
        pass_on(lax.slice_in_dim(left, steps * block // 2, steps * block, axis=0), -1),
    ]
    last, early = lax.optimization_barrier((last, rotate(ready, rotated)))
    rotated = rotate([(half, 0, last)] + later, [early])
    rotated = rotate([(half, 1, [other_core(x) for x in last])], [rotated])
    return (filtered, rotated)


def solution(mesh):
    return jax.shard_map(
        body,
        mesh=mesh,
        in_specs=(P("band", "grid"), P("grid", None), P(), P(), P(None, "band", None), P()),
        out_specs=(P("band", "grid"), P("band", "grid")),
        check_vma=False,
    )
```

```python
import functools

import jax
import jax.numpy as jnp
import ml_dtypes
import numpy as np
from jax import lax
from jax.experimental import pallas as pl
from jax.experimental.pallas import tpu as pltpu
from jax.sharding import PartitionSpec as P

NG = 96
KEEP = 32
EDGE_ENERGY = 1.3
NP = 64
LOW = 4
LANES = LOW * KEEP
QUAD = 4
GROUP = 4
MIB = 1024 * 1024

F32 = jnp.float32
BF16 = jnp.bfloat16


def cas(angle):
    return np.cos(angle) + np.sin(angle)


SIGNED = np.where(np.arange(KEEP) < KEEP // 2, np.arange(KEEP), np.arange(KEEP) - KEEP).astype(np.float64)
POINTS = 2.0 * np.pi * (np.arange(NP) + 0.5) / NP


def product_basis(points):
    return np.concatenate(
        [np.cos(points[:, None] * np.arange(KEEP)), np.sin(points[:, None] * np.arange(1, KEEP + 1))], axis=1
    )


PROJECT = np.linalg.solve(product_basis(POINTS).T, product_basis(2.0 * np.pi * np.arange(NG) / NG).T)
TABLE = cas(POINTS[:, None] * SIGNED[None, :]) / np.sqrt(NG)
Y_ORDER = np.arange(NP).reshape(NP // 2, 2).T.reshape(-1)
KX_ORDER = np.arange(KEEP).reshape(KEEP // LOW, LOW).T.reshape(-1)


ROW_SYN, ROW_ANA = 0, NP
ROW_Z_SYN = ROW_ANA + 2 * KEEP
ROW_Z_ANA = ROW_Z_SYN + 3 * LANES
ROW_PROJECT = ROW_Z_ANA + 2 * LANES


def halves(table):
    high = table.astype(np.float32).astype(ml_dtypes.bfloat16)
    low = (table - high.astype(np.float64)).astype(np.float32).astype(ml_dtypes.bfloat16)
    return high, low


def left_table(table):
    high, low = halves(table)
    return np.concatenate([high, low, high], axis=1)


def summed_table(table):
    high, low = halves(table)
    return np.concatenate(
        [np.concatenate([high, high], axis=1), np.concatenate([low, np.zeros_like(low)], axis=1)], axis=0
    )


def split(x):
    high = x.astype(BF16)
    return high, (x - high.astype(F32)).astype(BF16)


def stack(x):
    high, low = split(x)
    return jnp.concatenate([high, high, low], axis=0)


def times(table, parts):
    res = mm(table, stack(jnp.concatenate(parts, axis=1)))
    width = parts[0].shape[1]
    return [res[:, i * width:(i + 1) * width] for i in range(len(parts))]


def times_summed(table, parts):
    res = mm(table, jnp.concatenate(split(jnp.concatenate(parts, axis=1)), axis=0))
    half, width = res.shape[0] // 2, parts[0].shape[1]
    res = res[:half] + res[half:]
    return [res[:, i * width:(i + 1) * width] for i in range(len(parts))]


def mm(a, b):
    return jnp.dot(a, b, preferred_element_type=F32)


def sheet(shape, *parts):
    whole = np.zeros(shape, ml_dtypes.bfloat16)
    for row, lane, part in parts:
        whole[row:row + part.shape[0], lane:lane + part.shape[1]] = part
    return jnp.asarray(whole)


def lane_transpose(parts):
    lane = lax.broadcasted_iota(jnp.int32, (1, LANES), 1)
    second = (lane // 64) == 1
    odd = (lane // 32) % 2 == 1
    a, b, c, d = parts
    p0 = jnp.where(second, pltpu.roll(c, 64, 1), a)
    p2 = jnp.where(second, c, pltpu.roll(a, 64, 1))
    p1 = jnp.where(second, pltpu.roll(d, 64, 1), b)
    p3 = jnp.where(second, d, pltpu.roll(b, 64, 1))
    r0 = jnp.where(odd, pltpu.roll(p1, 32, 1), p0)
    r1 = jnp.where(odd, p1, pltpu.roll(p0, 96, 1))
    r2 = jnp.where(odd, pltpu.roll(p3, 32, 1), p2)
    r3 = jnp.where(odd, p3, pltpu.roll(p2, 96, 1))
    return [r0, r1, r2, r3]


def pack_kernel(slices, c_ref, *rest):
    outs, scratch = rest[:slices], rest[slices]
    rows = scratch.shape[0] // 8
    each = 8 // slices
    g = lax.axis_index("grid")
    for r in range(rows):
        scratch[pl.ds(r, 8, stride=rows), :] = c_ref[:, r * LANES:(r + 1) * LANES]
    for k in range(slices):
        dest = lax.rem(g + k, slices)
        start = pl.multiple_of(dest * (each * rows), each * rows)
        outs[k][...] = scratch[pl.ds(start, each * rows), :].reshape(each, rows, LANES)


def unpack_kernel(slices, *refs):
    ins, (out, scratch) = refs[:slices], refs[slices:]
    rows = scratch.shape[0] // 8
    each = 8 // slices
    g = lax.axis_index("grid")
    for k in range(slices):
        source = lax.rem(g + slices - k, slices)
        start = pl.multiple_of(source * (each * rows), each * rows)
        scratch[pl.ds(start, each * rows), :] = ins[k][...].reshape(each * rows, LANES)
    for r in range(rows):
        out[:, r * LANES:(r + 1) * LANES] = scratch[pl.ds(r, 8, stride=rows), :]


def project_kernel(ways, v_ref, tables, after, out_ref, first, second):
    planes = out_ref.shape[0]
    start = 0
    if ways > 1:
        start = pl.multiple_of(lax.rem(lax.axis_index("band"), ways) * planes, planes)
    z_high, z_low = tables[:NG, :LANES], tables[:NG, LANES:2 * LANES]
    group = 16
    for y0 in range(0, NG, group):
        x = jnp.concatenate(
            [v_ref[pl.ds(start, planes), (y0 + i) * NG:(y0 + i + 1) * NG] for i in range(group)], axis=0
        )
        high, low = split(x)
        first[y0 * planes:(y0 + group) * planes, :] = mm(high, z_high) + mm(high, z_low) + mm(low, z_high)
    y_table = tables[NG:NG + NP, :3 * NG]
    for p in range(0, planes, 2):
        x = jnp.concatenate([first[pl.ds(p + i, NG, stride=planes), :] for i in range(2)], axis=1)
        res, = times(y_table, [x])
        for i in range(2):
            second[pl.ds(p + i, NP, stride=planes), :] = res[:, i * LANES:(i + 1) * LANES]
    left = lax.broadcasted_iota(jnp.int32, (1, LANES), 1) < NP
    for j in range(NP // 2):
        even = second[2 * j * planes:(2 * j + 1) * planes, :]
        odd = second[(2 * j + 1) * planes:(2 * j + 2) * planes, :]
        out_ref[:, j * LANES:(j + 1) * LANES] = jnp.where(left, even, odd)


def synthesis_kernel(slices, ways, *refs):
    coeffs, pieces, (tables, who) = refs[:slices], refs[slices:slices + ways], refs[slices + ways:slices + ways + 2]
    c_all, field, tables_out, projection, who_out, z_first, x1, planes_now = refs[slices + ways + 2:]
    tables_out[...] = tables[...]
    who_out[...] = who[...]
    g = lax.axis_index("grid")
    each, rows, _ = coeffs[0].shape
    ky_local = KEEP // slices
    kx_high = KEEP // LOW
    for k in range(slices):
        source = lax.rem(g + slices - k, slices)
        parts = [coeffs[k][b] if b < each else jnp.zeros((rows, LANES), F32) for b in range(QUAD)]
        for low, part in enumerate(lane_transpose(parts)):
            c_all[pl.ds(source * ky_local, ky_local), low * kx_high:(low + 1) * kx_high, :] = part.reshape(
                ky_local, kx_high, LANES
            )
    project_x(pieces, g, tables, planes_now, lambda lanes, value: put_lanes(projection, lanes, value))
    synthesize(c_all, tables, z_first, x1, lambda x, values: put(field, x * NP, jnp.concatenate(values, axis=0)))


def put_lanes(ref, lanes, value):
    ref[:, lanes] = value


def project_x(pieces, source, tables, planes_now, give):
    ways = len(pieces)
    planes = pieces[0].shape[0]
    slot = planes_now.shape[0] // ways
    core = lax.rem(lax.axis_index("band"), ways)
    if slot != planes:
        planes_now[...] = jnp.zeros_like(planes_now)
    for w in range(ways):
        start = pl.multiple_of(lax.rem(core + w, ways) * slot, slot)
        planes_now[pl.ds(start, planes), :] = pieces[w][...]
    row = pl.multiple_of(ROW_PROJECT + source * NP, NP)
    table = tables[pl.ds(row, NP), :][:, :3 * ways * slot]
    width = 512
    for lane in range(0, NP * NP, width):
        give(slice(lane, lane + width), mm(table, stack(planes_now[:, lane:lane + width])))


def put(ref, row, value):
    ref[row:row + value.shape[0], :] = value


def put_wide(ref, row, value):
    for h in range(2):
        ref[h, row:row + value.shape[0], :] = value[:, h * LANES:(h + 1) * LANES]


def wide(ref, start, size, stride):
    return jnp.concatenate([ref[h, pl.ds(start, size, stride=stride), :] for h in range(2)], axis=1)


def synthesize(u_all, tables, z_first, x1, give):
    z_syn = tables[ROW_Z_SYN:ROW_Z_SYN + 3 * LANES, :2 * LANES]
    group = 8
    for ky in range(0, KEEP, group):
        high, low = split(u_all[ky:ky + group].reshape(group * KEEP, LANES))
        put(z_first, ky * KEEP, mm(jnp.concatenate([high, high, low], axis=1), z_syn))
    xs = tables[ROW_SYN:ROW_SYN + NP, :3 * KEEP]
    for ky in range(0, KEEP, GROUP):
        parts = [z_first[(ky + i) * KEEP:(ky + i + 1) * KEEP, :] for i in range(GROUP)]
        for i, res in enumerate(times(xs, parts)):
            put_wide(x1, (ky + i) * NP, res)
    ys = tables[ROW_SYN:ROW_SYN + NP, LANES:LANES + 3 * KEEP]
    for x in range(0, NP, GROUP):
        give(x, times(ys, [wide(x1, x + i, KEEP, NP) for i in range(GROUP)]))


def filter_kernel(slices, ways, *refs):
    c_all, field, projection = refs[:3]
    pieces = refs[3:3 + (slices - 1) * ways]
    refs = refs[3 + (slices - 1) * ways:]
    lower, upper, tables = refs[:3]
    outs, spread = refs[3:3 + slices], refs[3 + slices]
    planes_now, total, vx, u_all, z_first, x1, y2, packed = refs[4 + slices:]
    g = lax.axis_index("grid")
    each, rows, _ = outs[0].shape
    kx_high = KEEP // LOW

    def add(lanes, value):
        total[:, lanes] += value

    def finish_projection(lanes, value):
        value = value + (projection if slices == 2 else total)[:, lanes]
        for j in range(value.shape[1] // LANES):
            put(vx, (lanes.start // LANES + j) * NP, value[:, j * LANES:(j + 1) * LANES])

    if slices > 2:
        total[...] = projection[...]
    for k in range(1, slices):
        project_x(
            pieces[(k - 1) * ways:k * ways],
            lax.rem(g + slices - k, slices),
            tables,
            planes_now,
            finish_projection if k == slices - 1 else add,
        )
    left = lax.broadcasted_iota(jnp.int32, (1, LANES), 1) < NP

    low_edge = jnp.full((1, LANES), lower[0], F32)
    high_edge = jnp.full((1, LANES), upper[0], F32)
    center = (low_edge + high_edge) * 0.5
    half_width = (high_edge - low_edge) * 0.5

    row = lax.broadcasted_iota(jnp.int32, (KEEP, LANES), 0)
    lane = lax.broadcasted_iota(jnp.int32, (KEEP, LANES), 1)
    kx = row % kx_high * LOW + row // kx_high
    kz = lane % KEEP
    signed = [jnp.where(k < KEEP // 2, k, k - KEEP).astype(F32) for k in (kx, kz)]
    square = signed[0] * signed[0] + signed[1] * signed[1]

    z_ana = tables[ROW_Z_ANA:ROW_Z_ANA + 2 * LANES, :2 * LANES]
    ya = tables[ROW_ANA:ROW_ANA + 2 * KEEP, :2 * NP]
    xa = tables[ROW_ANA:ROW_ANA + 2 * KEEP, 2 * NP:4 * NP]

    def weigh(x, values):
        parts = []
        for i, value in enumerate(values):
            local = vx[pl.ds(x + i, NP // 2, stride=NP), :]
            turned = pltpu.roll(local, NP, 1)
            local = jnp.concatenate([jnp.where(left, local, turned), jnp.where(left, turned, local)], axis=0)
            parts.append(value * jnp.concatenate([local, local], axis=1))
        for i, res in enumerate(times_summed(ya, parts)):
            put_wide(y2, (x + i) * KEEP, res)

    def finish(u, scale, back):
        for ky in range(0, KEEP, GROUP):
            res = times_summed(xa, [wide(y2, ky + i, NP, KEEP) for i in range(GROUP)])
            put(z_first, ky * KEEP, jnp.concatenate(res, axis=0))
        group = 8
        for ky in range(0, KEEP, group):
            high, low = split(z_first[ky * KEEP:(ky + group) * KEEP, :])
            twice = mm(high, z_ana)
            res = twice[:, :LANES] + twice[:, LANES:] + mm(low, z_ana[:, :LANES])
            for i in range(group):
                kinetic = EDGE_ENERGY * ((square + SIGNED[ky + i] ** 2) * (1.0 / (KEEP // 2) ** 2))
                now = u[ky + i]
                out = scale * (kinetic * now + res[i * KEEP:(i + 1) * KEEP, :] - center * now)
                u_all[ky + i] = out - c_all[ky + i] if back else out

    for x in range(0, NP, GROUP):
        weigh(x, [field[(x + i) * NP:(x + i + 1) * NP, :] for i in range(GROUP)])
    finish(c_all, 1.0 / half_width, False)
    synthesize(u_all, tables, z_first, x1, weigh)
    finish(u_all, 2.0 / half_width, True)

    parts = [
        u_all[:, low * kx_high:(low + 1) * kx_high, :].reshape(KEEP * kx_high, LANES) for low in range(LOW)
    ]
    for b, part in enumerate(lane_transpose(parts)[:each]):
        packed[b] = part
    for k in range(slices):
        dest = lax.rem(g + k, slices)
        start = pl.multiple_of(dest * rows, rows)
        for b in range(each):
            outs[k][b] = packed[b, pl.ds(start, rows), :]
    run = spread.shape[1] // each
    groups = rows // run
    for dest in range(groups * slices):
        start = (dest % slices) * rows + (dest // slices) * run
        for b in range(each):
            spread[dest, b * run:(b + 1) * run, :] = packed[b, start:start + run, :]


def select_kernel(owners, came, *outs):
    steps = owners.shape[1]
    run = outs[0].shape[1] // LANES
    each = steps // len(outs)
    block = outs[0].shape[0] // each
    for s in range(steps):
        out, row = outs[s // each], s % each * block
        for r in range(run):
            start = owners[0, s] * (block * run) + r
            out[row:row + block, r * LANES:(r + 1) * LANES] = came[pl.ds(start, block, stride=run), :]


def rotate_kernel(moves, chips, continued, keep, table, *refs):
    refs = list(refs)
    results, sems = refs[-2:]
    together = None
    pieces = []
    for _, _, parts in moves:
        if parts < 0:
            together = refs.pop(0) if together is None else together
            pieces.append([together.at[-1 - parts]])
        else:
            pieces.append([refs.pop(0) for _ in range(parts)])
    if continued:
        refs.pop(0)
    out, kept = refs[0], refs[1] if keep else None
    band = lax.axis_index("band")
    chip, core = band // 2, lax.rem(band, 2)
    position = jnp.where(lax.rem(chip, 2) == 0, chip // 2, chips - 1 - chip // 2)
    slots, _, width = results.shape
    left = table[...]
    stores = []
    for j, ((offset, flip, _), parts) in enumerate(zip(moves, pieces)):
        block = jnp.concatenate([part[...] for part in parts], axis=0)
        if j < keep:
            kept[j] = block
        res = mm(left, stack(block))
        if j >= slots:
            stores[j - slots].wait()
        results[j % slots] = res
        place = lax.rem(position + (chips + offset), chips)
        owner = jnp.where(place < chips // 2, 2 * place, 2 * (chips - 1 - place) + 1)
        start = pl.multiple_of((2 * owner + (core if flip == 0 else 1 - core)) * width, width)
        store = pltpu.make_async_copy(results.at[j % slots], out.at[:, pl.ds(start, width)], sems.at[j % slots])
        store.start()
        stores.append(store)
    for store in stores[-slots:]:
        store.wait()


def params(mib):
    return pltpu.CompilerParams(vmem_limit_bytes=mib * MIB)


def in_vmem(count):
    return [pl.BlockSpec(memory_space=pltpu.VMEM)] * count


def body(block_coeffs, potential, lower_edge, upper_edge, rotation, owners):
    slices = lax.axis_size("grid")
    groups = lax.axis_size("band")
    block, cols = block_coeffs.shape
    rows = cols // LANES
    each = block // slices
    steps = rotation.shape[0]
    ways = 2 if potential.shape[0] % 16 == 0 else 1
    planes = potential.shape[0] // ways
    slot = -(-planes // 8) * 8

    def shift(x, k):
        return lax.ppermute(x, "grid", [(i, (i + k) % slices) for i in range(slices)])

    def shift_diagonal(x, k):
        pairs = [
            (i * slices + j, (i ^ 1) * slices + (j + k) % slices) for i in range(groups) for j in range(slices)
        ]
        return lax.ppermute(x, ("band", "grid"), pairs)

    def other_core(x):
        return lax.ppermute(x, "band", [(i, i ^ 1) for i in range(groups)])

    piece = jax.ShapeDtypeStruct((each, rows, LANES), F32)
    packed = pl.pallas_call(
        functools.partial(pack_kernel, slices),
        out_shape=[piece] * slices,
        in_specs=in_vmem(1),
        out_specs=in_vmem(slices),
        scratch_shapes=[pltpu.VMEM((block * rows, LANES), F32)],
        compiler_params=params(8),
        name="pack",
    )(block_coeffs)
    coeffs = [packed[0]] + [shift(packed[k], k) for k in range(1, slices)]

    z_high, z_low = halves(np.concatenate([PROJECT.T, PROJECT.T], axis=1))
    project_tables = sheet(
        (NG + NP, 3 * LANES), (0, 0, z_high), (0, LANES, z_low), (NG, 0, left_table(PROJECT))
    )
    projected = pl.pallas_call(
        functools.partial(project_kernel, ways),
        out_shape=jax.ShapeDtypeStruct((planes, NP * NP), F32),
        in_specs=in_vmem(2) + [pl.BlockSpec(memory_space=pl.ANY)],
        out_specs=pl.BlockSpec(memory_space=pltpu.VMEM),
        scratch_shapes=[pltpu.VMEM((NG * planes, LANES), F32), pltpu.VMEM((NP * planes, LANES), F32)],
        compiler_params=params(12),
        name="project",
    )(potential, project_tables, packed[0])
    projected, coeffs = lax.optimization_barrier((projected, coeffs))
    own_pieces = [projected, other_core(projected)] if ways > 1 else [projected]

    eye = np.eye(QUAD)
    z_high, z_low = halves(np.kron(eye, TABLE.T))
    back_high, back_low = halves(np.kron(eye, TABLE))
    slots = np.zeros((NP, slices, ways, slot))
    slots[..., :planes] = PROJECT.reshape(NP, slices, ways, planes)
    tables = sheet(
        (ROW_PROJECT + slices * NP, 2 * LANES),
        (ROW_SYN, 0, left_table(TABLE[:, KX_ORDER])),
        (ROW_SYN, LANES, left_table(TABLE[Y_ORDER])),
        (ROW_ANA, 0, summed_table(TABLE[Y_ORDER].T)),
        (ROW_ANA, 2 * NP, summed_table(TABLE[:, KX_ORDER].T)),
        (ROW_Z_SYN, 0, np.concatenate([z_high, z_low, z_high], axis=0)),
        (ROW_Z_ANA, 0, np.concatenate([back_high, back_low], axis=1)),
        *[(ROW_PROJECT + k * NP, 0, left_table(slots[:, k].reshape(NP, -1))) for k in range(slices)],
    )
    cube = jax.ShapeDtypeStruct((KEEP, KEEP, LANES), F32)
    c_all, field, tables, projection, owners = pl.pallas_call(
        functools.partial(synthesis_kernel, slices, ways),
        out_shape=[
            cube,
            jax.ShapeDtypeStruct((NP * NP, 2 * LANES), F32),
            jax.ShapeDtypeStruct(tables.shape, tables.dtype),
            jax.ShapeDtypeStruct((NP, NP * NP), F32),
            jax.ShapeDtypeStruct((1, steps), jnp.int32),
        ],
        in_specs=in_vmem(slices + ways + 2),
        out_specs=in_vmem(5),
        scratch_shapes=[
            pltpu.VMEM((KEEP * KEEP, 2 * LANES), F32),
            pltpu.VMEM((2, KEEP * NP, LANES), F32),
            pltpu.VMEM((ways * slot, NP * NP), F32),
        ],
        compiler_params=params(20),
        cost_estimate=pl.CostEstimate(flops=1, bytes_accessed=1, transcendentals=0),
        name="synthesis",
    )(*coeffs, *own_pieces, tables, owners.reshape(1, steps))

    pieces = []
    for k in range(1, slices):
        if ways == 1:
            pieces.append(shift(projected, k))
        else:
            came, c_all, field = lax.optimization_barrier((shift_diagonal(projected, k), c_all, field))
            pieces += [other_core(came), came]

    *filtered_pieces, spread = pl.pallas_call(
        functools.partial(filter_kernel, slices, ways),
        out_shape=[piece] * slices
        + [jax.ShapeDtypeStruct((groups * slices, each * rows // groups, LANES), F32)],
        in_specs=in_vmem(3 + (slices - 1) * ways) + [pl.BlockSpec(memory_space=pltpu.SMEM)] * 2 + in_vmem(1),
        out_specs=in_vmem(slices + 1),
        scratch_shapes=[
            pltpu.VMEM((ways * slot, NP * NP), F32),
            pltpu.VMEM((NP if slices > 2 else 8, NP * NP), F32),
            pltpu.VMEM((NP * NP // 2, LANES), F32),
            pltpu.VMEM((KEEP, KEEP, LANES), F32),
            pltpu.VMEM((KEEP * KEEP, 2 * LANES), F32),
            pltpu.VMEM((2, KEEP * NP, LANES), F32),
            pltpu.VMEM((2, KEEP * NP, LANES), F32),
            pltpu.VMEM((each, KEEP * KEEP // LOW, LANES), F32),
        ],
        compiler_params=params(28),
        name="chebyshev",
    )(c_all, field, projection, *pieces, lower_edge, upper_edge, tables)
    arrived = [filtered_pieces[0]] + [shift(filtered_pieces[k], k) for k in range(1, slices)]
    filtered = pl.pallas_call(
        functools.partial(unpack_kernel, slices),
        out_shape=jax.ShapeDtypeStruct((block, cols), F32),
        in_specs=in_vmem(slices),
        out_specs=pl.BlockSpec(memory_space=pltpu.VMEM),
        scratch_shapes=[pltpu.VMEM((block * rows, LANES), F32)],
        compiler_params=params(8),
        cost_estimate=pl.CostEstimate(flops=1, bytes_accessed=1, transcendentals=0),
        name="unpack",
    )(*arrived)

    flat = jnp.transpose(rotation, (1, 0, 2)).reshape(rotation.shape[1], steps * block)
    high, low = split(flat)
    table = jnp.concatenate([high, low, high], axis=1)

    came = lax.all_to_all(spread, ("band", "grid"), split_axis=0, concat_axis=0, tiled=True)
    came, table = lax.optimization_barrier((came, table))
    width = cols // groups
    mine = pl.pallas_call(
        select_kernel,
        out_shape=[jax.ShapeDtypeStruct((steps * block // 2, width), F32)] * 2,
        in_specs=[pl.BlockSpec(memory_space=pltpu.SMEM), pl.BlockSpec(memory_space=pltpu.VMEM)],
        out_specs=in_vmem(2),
        compiler_params=params(8),
        name="select",
    )(owners, came.reshape(-1, LANES))

    chips = groups // 2
    ring = list(range(0, chips, 2)) + list(range(1, chips, 2))[::-1]

    def pass_on(x, step, cross=0):
        pairs = [
            (2 * ring[p] + c, 2 * ring[(p + step) % chips] + (c ^ cross)) for p in range(chips) for c in range(2)
        ]
        return lax.ppermute(x, "band", pairs)

    rotated_shape = jax.ShapeDtypeStruct((rotation.shape[1], cols), F32)

    def rotate(moves, before, keep=0):
        arrays, plan = [], []
        for offset, flip, parts in moves:
            if isinstance(parts, tuple):
                arrays += parts[:1] if parts[1] == 0 else []
                plan.append((offset, flip, -1 - parts[1]))
            else:
                arrays += parts
                plan.append((offset, flip, len(parts)))
        depth = min(3, len(moves))
        kept = [jax.ShapeDtypeStruct((keep, steps * block, width), F32)] if keep else []
        return pl.pallas_call(
            functools.partial(rotate_kernel, tuple(plan), chips, bool(before), keep),
            out_shape=[jax.ShapeDtypeStruct((rotation.shape[1], cols), F32)] + kept,
            in_specs=in_vmem(1 + len(arrays)) + [pl.BlockSpec(memory_space=pl.ANY)] * len(before),
            out_specs=[pl.BlockSpec(memory_space=pl.ANY)] + in_vmem(len(kept)),
            scratch_shapes=[
                pltpu.VMEM((depth, rotation.shape[1], width), F32),
                pltpu.SemaphoreType.DMA((depth,)),
            ],
            input_output_aliases={len(arrays) + 1: 0} if before else {},
            compiler_params=params(16),
            cost_estimate=pl.CostEstimate(flops=1_000_000_000, bytes_accessed=4_000_000, transcendentals=0),
            name="rotate",
        )(table, *arrays, *before)

    half = chips // 2
    right, left = list(mine), list(mine)
    own = [(0, 0, list(mine))]
    for k in range(1, half):
        right, left = [pass_on(x, 1) for x in right], [pass_on(x, -1) for x in left]
        if k == half - 2:
            filtered, left[1] = lax.optimization_barrier((filtered, left[1]))
        if k == half - 1:
            early, kept = rotate(own, [], len(own))
            right, left, early, kept = lax.optimization_barrier((right, left, early, kept))
            together = other_core(kept)
            ready = [(offset, 1, (together, i)) for i, (offset, _, _) in enumerate(own)]
            own = []
        own += [(-k, 0, right), (k, 0, left)]
    last = [pass_on(right[0], 1), pass_on(left[1], -1)]
    crossed = [pass_on(right[0], 1, 1), pass_on(left[1], -1, 1)]
    early, kept = rotate(own + ready, [early], len(own))
    last, crossed, early, kept = lax.optimization_barrier((last, crossed, early, kept))
    together = other_core(kept)
    later = [(offset, 1, (together, i)) for i, (offset, _, _) in enumerate(own)]
    rotated, = rotate([(half, 0, last), (half, 1, crossed)], [early])
    rotated, = rotate(later, [rotated])
    return (filtered, rotated)


def solution(mesh):
    return jax.shard_map(
        body,
        mesh=mesh,
        in_specs=(P("band", "grid"), P("grid", None), P(), P(), P(None, "band", None), P()),
        out_specs=(P("band", "grid"), P("band", "grid")),
        check_vma=False,
    )
```

```python
import functools

import jax
import jax.numpy as jnp
import ml_dtypes
import numpy as np
from jax import lax
from jax.experimental import pallas as pl
from jax.experimental.pallas import tpu as pltpu
from jax.sharding import PartitionSpec as P

NG = 96
KEEP = 32
EDGE_ENERGY = 1.3
NP = 64
LOW = 4
LANES = LOW * KEEP
QUAD = 4
GROUP = 16
MIB = 1024 * 1024

F32 = jnp.float32
BF16 = jnp.bfloat16


def cas(angle):
    return np.cos(angle) + np.sin(angle)


SIGNED = np.where(np.arange(KEEP) < KEEP // 2, np.arange(KEEP), np.arange(KEEP) - KEEP).astype(np.float64)
POINTS = 2.0 * np.pi * (np.arange(NP) + 0.5) / NP


def product_basis(points):
    return np.concatenate(
        [np.cos(points[:, None] * np.arange(KEEP)), np.sin(points[:, None] * np.arange(1, KEEP + 1))], axis=1
    )


PROJECT = np.linalg.solve(product_basis(POINTS).T, product_basis(2.0 * np.pi * np.arange(NG) / NG).T)
TABLE = cas(POINTS[:, None] * SIGNED[None, :]) / np.sqrt(NG)
Y_ORDER = np.arange(NP).reshape(NP // 2, 2).T.reshape(-1)
KX_ORDER = np.arange(KEEP).reshape(KEEP // LOW, LOW).T.reshape(-1)


ROW_SYN, ROW_ANA = 0, NP
ROW_Z_SYN = ROW_ANA + 2 * KEEP
ROW_Z_ANA = ROW_Z_SYN + 3 * LANES
ROW_PROJECT = ROW_Z_ANA + 2 * LANES


def halves(table):
    high = table.astype(np.float32).astype(ml_dtypes.bfloat16)
    low = (table - high.astype(np.float64)).astype(np.float32).astype(ml_dtypes.bfloat16)
    return high, low


def left_table(table):
    high, low = halves(table)
    return np.concatenate([high, low, high], axis=1)


def summed_table(table):
    high, low = halves(table)
    return np.concatenate(
        [np.concatenate([high, high], axis=1), np.concatenate([low, np.zeros_like(low)], axis=1)], axis=0
    )


def split(x):
    high = x.astype(BF16)
    return high, (x - high.astype(F32)).astype(BF16)


def stack(x):
    high, low = split(x)
    return jnp.concatenate([high, high, low], axis=0)


def times(table, parts):
    res = mm(table, stack(jnp.concatenate(parts, axis=1)))
    width = parts[0].shape[1]
    return [res[:, i * width:(i + 1) * width] for i in range(len(parts))]


def times_summed(table, parts):
    res = mm(table, jnp.concatenate(split(jnp.concatenate(parts, axis=1)), axis=0))
    half, width = res.shape[0] // 2, parts[0].shape[1]
    res = res[:half] + res[half:]
    return [res[:, i * width:(i + 1) * width] for i in range(len(parts))]


def mm(a, b):
    return jnp.dot(a, b, preferred_element_type=F32)


def sheet(shape, *parts):
    whole = np.zeros(shape, ml_dtypes.bfloat16)
    for row, lane, part in parts:
        whole[row:row + part.shape[0], lane:lane + part.shape[1]] = part
    return jnp.asarray(whole)


def lane_transpose(parts):
    lane = lax.broadcasted_iota(jnp.int32, (1, LANES), 1)
    second = (lane // 64) == 1
    odd = (lane // 32) % 2 == 1
    a, b, c, d = parts
    p0 = jnp.where(second, pltpu.roll(c, 64, 1), a)
    p2 = jnp.where(second, c, pltpu.roll(a, 64, 1))
    p1 = jnp.where(second, pltpu.roll(d, 64, 1), b)
    p3 = jnp.where(second, d, pltpu.roll(b, 64, 1))
    r0 = jnp.where(odd, pltpu.roll(p1, 32, 1), p0)
    r1 = jnp.where(odd, p1, pltpu.roll(p0, 96, 1))
    r2 = jnp.where(odd, pltpu.roll(p3, 32, 1), p2)
    r3 = jnp.where(odd, p3, pltpu.roll(p2, 96, 1))
    return [r0, r1, r2, r3]


def pack_kernel(slices, c_ref, *rest):
    outs, scratch = rest[:slices], rest[slices]
    rows = scratch.shape[0] // 8
    each = 8 // slices
    g = lax.axis_index("grid")
    for r in range(rows):
        scratch[pl.ds(r, 8, stride=rows), :] = c_ref[:, r * LANES:(r + 1) * LANES]
    for k in range(slices):
        dest = lax.rem(g + k, slices)
        start = pl.multiple_of(dest * (each * rows), each * rows)
        outs[k][...] = scratch[pl.ds(start, each * rows), :].reshape(each, rows, LANES)


def unpack_kernel(slices, *refs):
    ins, (out, scratch) = refs[:slices], refs[slices:]
    rows = scratch.shape[0] // 8
    each = 8 // slices
    g = lax.axis_index("grid")
    for k in range(slices):
        source = lax.rem(g + slices - k, slices)
        start = pl.multiple_of(source * (each * rows), each * rows)
        scratch[pl.ds(start, each * rows), :] = ins[k][...].reshape(each * rows, LANES)
    for r in range(rows):
        out[:, r * LANES:(r + 1) * LANES] = scratch[pl.ds(r, 8, stride=rows), :]


def project_kernel(ways, v_ref, tables, after, out_ref, first, second):
    planes = out_ref.shape[0]
    start = 0
    if ways > 1:
        start = pl.multiple_of(lax.rem(lax.axis_index("band"), ways) * planes, planes)
    z_high, z_low = tables[:NG, :LANES], tables[:NG, LANES:2 * LANES]
    group = 16
    for y0 in range(0, NG, group):
        x = jnp.concatenate(
            [v_ref[pl.ds(start, planes), (y0 + i) * NG:(y0 + i + 1) * NG] for i in range(group)], axis=0
        )
        high, low = split(x)
        first[y0 * planes:(y0 + group) * planes, :] = mm(high, z_high) + mm(high, z_low) + mm(low, z_high)
    y_table = tables[NG:NG + NP, :3 * NG]
    for p in range(0, planes, 2):
        x = jnp.concatenate([first[pl.ds(p + i, NG, stride=planes), :] for i in range(2)], axis=1)
        res, = times(y_table, [x])
        for i in range(2):
            second[pl.ds(p + i, NP, stride=planes), :] = res[:, i * LANES:(i + 1) * LANES]
    left = lax.broadcasted_iota(jnp.int32, (1, LANES), 1) < NP
    for j in range(NP // 2):
        even = second[2 * j * planes:(2 * j + 1) * planes, :]
        odd = second[(2 * j + 1) * planes:(2 * j + 2) * planes, :]
        out_ref[:, j * LANES:(j + 1) * LANES] = jnp.where(left, even, odd)


def synthesis_kernel(slices, ways, *refs):
    coeffs, pieces, (tables, who) = refs[:slices], refs[slices:slices + ways], refs[slices + ways:slices + ways + 2]
    c_all, field, tables_out, projection, who_out, z_first, x1, planes_now = refs[slices + ways + 2:]
    tables_out[...] = tables[...]
    who_out[...] = who[...]
    g = lax.axis_index("grid")
    each, rows, _ = coeffs[0].shape
    ky_local = KEEP // slices
    kx_high = KEEP // LOW
    for k in range(slices):
        source = lax.rem(g + slices - k, slices)
        parts = [coeffs[k][b] if b < each else jnp.zeros((rows, LANES), F32) for b in range(QUAD)]
        for low, part in enumerate(lane_transpose(parts)):
            c_all[pl.ds(source * ky_local, ky_local), low * kx_high:(low + 1) * kx_high, :] = part.reshape(
                ky_local, kx_high, LANES
            )
    project_x(pieces, g, tables, planes_now, lambda lanes, value: put_lanes(projection, lanes, value))
    synthesize(c_all, tables, z_first, x1, lambda x, values: put(field, x * NP, jnp.concatenate(values, axis=0)))


def put_lanes(ref, lanes, value):
    ref[:, lanes] = value


def project_x(pieces, source, tables, planes_now, give):
    ways = len(pieces)
    planes = pieces[0].shape[0]
    slot = planes_now.shape[0] // ways
    core = lax.rem(lax.axis_index("band"), ways)
    if slot != planes:
        planes_now[...] = jnp.zeros_like(planes_now)
    for w in range(ways):
        start = pl.multiple_of(lax.rem(core + w, ways) * slot, slot)
        planes_now[pl.ds(start, planes), :] = pieces[w][...]
    row = pl.multiple_of(ROW_PROJECT + source * NP, NP)
    table = tables[pl.ds(row, NP), :][:, :3 * ways * slot]
    width = 512
    for lane in range(0, NP * NP, width):
        give(slice(lane, lane + width), mm(table, stack(planes_now[:, lane:lane + width])))


def put(ref, row, value):
    ref[row:row + value.shape[0], :] = value


def put_wide(ref, row, value):
    for h in range(2):
        ref[h, row:row + value.shape[0], :] = value[:, h * LANES:(h + 1) * LANES]


def wide(ref, start, size, stride):
    return jnp.concatenate([ref[h, pl.ds(start, size, stride=stride), :] for h in range(2)], axis=1)


def synthesize(u_all, tables, z_first, x1, give):
    z_syn = tables[ROW_Z_SYN:ROW_Z_SYN + 3 * LANES, :2 * LANES]
    group = 8
    for ky in range(0, KEEP, group):
        high, low = split(u_all[ky:ky + group].reshape(group * KEEP, LANES))
        put(z_first, ky * KEEP, mm(jnp.concatenate([high, high, low], axis=1), z_syn))
    xs = tables[ROW_SYN:ROW_SYN + NP, :3 * KEEP]
    for ky in range(0, KEEP, GROUP):
        parts = [z_first[(ky + i) * KEEP:(ky + i + 1) * KEEP, :] for i in range(GROUP)]
        for i, res in enumerate(times(xs, parts)):
            put_wide(x1, (ky + i) * NP, res)
    ys = tables[ROW_SYN:ROW_SYN + NP, LANES:LANES + 3 * KEEP]
    for x in range(0, NP, GROUP):
        give(x, times(ys, [wide(x1, x + i, KEEP, NP) for i in range(GROUP)]))


def filter_kernel(slices, ways, *refs):
    c_all, field, projection = refs[:3]
    pieces = refs[3:3 + (slices - 1) * ways]
    refs = refs[3 + (slices - 1) * ways:]
    lower, upper, tables = refs[:3]
    outs, spread = refs[3:3 + slices], refs[3 + slices]
    planes_now, total, vx, u_all, z_first, x1, y2, packed = refs[4 + slices:]
    g = lax.axis_index("grid")
    each, rows, _ = outs[0].shape
    kx_high = KEEP // LOW

    def add(lanes, value):
        total[:, lanes] += value

    def finish_projection(lanes, value):
        value = value + (projection if slices == 2 else total)[:, lanes]
        for j in range(value.shape[1] // LANES):
            put(vx, (lanes.start // LANES + j) * NP, value[:, j * LANES:(j + 1) * LANES])

    if slices > 2:
        total[...] = projection[...]
    for k in range(1, slices):
        project_x(
            pieces[(k - 1) * ways:k * ways],
            lax.rem(g + slices - k, slices),
            tables,
            planes_now,
            finish_projection if k == slices - 1 else add,
        )
    left = lax.broadcasted_iota(jnp.int32, (1, LANES), 1) < NP

    low_edge = jnp.full((1, LANES), lower[0], F32)
    high_edge = jnp.full((1, LANES), upper[0], F32)
    center = (low_edge + high_edge) * 0.5
    half_width = (high_edge - low_edge) * 0.5

    row = lax.broadcasted_iota(jnp.int32, (KEEP, LANES), 0)
    lane = lax.broadcasted_iota(jnp.int32, (KEEP, LANES), 1)
    kx = row % kx_high * LOW + row // kx_high
    kz = lane % KEEP
    signed = [jnp.where(k < KEEP // 2, k, k - KEEP).astype(F32) for k in (kx, kz)]
    square = signed[0] * signed[0] + signed[1] * signed[1]

    z_ana = tables[ROW_Z_ANA:ROW_Z_ANA + 2 * LANES, :2 * LANES]
    ya = tables[ROW_ANA:ROW_ANA + 2 * KEEP, :2 * NP]
    xa = tables[ROW_ANA:ROW_ANA + 2 * KEEP, 2 * NP:4 * NP]

    def weigh(x, values):
        parts = []
        for i, value in enumerate(values):
            local = vx[pl.ds(x + i, NP // 2, stride=NP), :]
            turned = pltpu.roll(local, NP, 1)
            local = jnp.concatenate([jnp.where(left, local, turned), jnp.where(left, turned, local)], axis=0)
            parts.append(value * jnp.concatenate([local, local], axis=1))
        for i, res in enumerate(times_summed(ya, parts)):
            put_wide(y2, (x + i) * KEEP, res)

    def finish(u, scale, back):
        for ky in range(0, KEEP, GROUP):
            res = times_summed(xa, [wide(y2, ky + i, NP, KEEP) for i in range(GROUP)])
            put(z_first, ky * KEEP, jnp.concatenate(res, axis=0))
        group = 8
        for ky in range(0, KEEP, group):
            high, low = split(z_first[ky * KEEP:(ky + group) * KEEP, :])
            twice = mm(high, z_ana)
            res = twice[:, :LANES] + twice[:, LANES:] + mm(low, z_ana[:, :LANES])
            for i in range(group):
                kinetic = EDGE_ENERGY * ((square + SIGNED[ky + i] ** 2) * (1.0 / (KEEP // 2) ** 2))
                now = u[ky + i]
                out = scale * (kinetic * now + res[i * KEEP:(i + 1) * KEEP, :] - center * now)
                u_all[ky + i] = out - c_all[ky + i] if back else out

    for x in range(0, NP, GROUP):
        weigh(x, [field[(x + i) * NP:(x + i + 1) * NP, :] for i in range(GROUP)])
    finish(c_all, 1.0 / half_width, False)
    synthesize(u_all, tables, z_first, x1, weigh)
    finish(u_all, 2.0 / half_width, True)

    parts = [
        u_all[:, low * kx_high:(low + 1) * kx_high, :].reshape(KEEP * kx_high, LANES) for low in range(LOW)
    ]
    for b, part in enumerate(lane_transpose(parts)[:each]):
        packed[b] = part
    for k in range(slices):
        dest = lax.rem(g + k, slices)
        start = pl.multiple_of(dest * rows, rows)
        for b in range(each):
            outs[k][b] = packed[b, pl.ds(start, rows), :]
    run = spread.shape[1] // each
    groups = rows // run
    for dest in range(groups * slices):
        start = (dest % slices) * rows + (dest // slices) * run
        for b in range(each):
            spread[dest, b * run:(b + 1) * run, :] = packed[b, start:start + run, :]


def select_kernel(owners, came, *outs):
    steps = owners.shape[1]
    run = outs[0].shape[1] // LANES
    each = steps // len(outs)
    block = outs[0].shape[0] // each
    for s in range(steps):
        out, row = outs[s // each], s % each * block
        for r in range(run):
            start = owners[0, s] * (block * run) + r
            out[row:row + block, r * LANES:(r + 1) * LANES] = came[pl.ds(start, block, stride=run), :]


def rotate_kernel(moves, chips, continued, keep, table, *refs):
    refs = list(refs)
    results, sems = refs[-2:]
    together = None
    pieces = []
    for _, _, parts in moves:
        if parts < 0:
            together = refs.pop(0) if together is None else together
            pieces.append([together.at[-1 - parts]])
        else:
            pieces.append([refs.pop(0) for _ in range(parts)])
    if continued:
        refs.pop(0)
    out, kept = refs[0], refs[1] if keep else None
    band = lax.axis_index("band")
    chip, core = band // 2, lax.rem(band, 2)
    position = jnp.where(lax.rem(chip, 2) == 0, chip // 2, chips - 1 - chip // 2)
    slots, _, width = results.shape
    left = table[...]
    stores = []
    for j, ((offset, flip, _), parts) in enumerate(zip(moves, pieces)):
        block = jnp.concatenate([part[...] for part in parts], axis=0)
        if j < keep:
            kept[j] = block
        res = mm(left, stack(block))
        if j >= slots:
            stores[j - slots].wait()
        results[j % slots] = res
        place = lax.rem(position + (chips + offset), chips)
        owner = jnp.where(place < chips // 2, 2 * place, 2 * (chips - 1 - place) + 1)
        start = pl.multiple_of((2 * owner + (core if flip == 0 else 1 - core)) * width, width)
        store = pltpu.make_async_copy(results.at[j % slots], out.at[:, pl.ds(start, width)], sems.at[j % slots])
        store.start()
        stores.append(store)
    for store in stores[-slots:]:
        store.wait()


def params(mib):
    return pltpu.CompilerParams(vmem_limit_bytes=mib * MIB)


def in_vmem(count):
    return [pl.BlockSpec(memory_space=pltpu.VMEM)] * count


def body(block_coeffs, potential, lower_edge, upper_edge, rotation, owners):
    slices = lax.axis_size("grid")
    groups = lax.axis_size("band")
    block, cols = block_coeffs.shape
    rows = cols // LANES
    each = block // slices
    steps = rotation.shape[0]
    ways = 2 if potential.shape[0] % 16 == 0 else 1
    planes = potential.shape[0] // ways
    slot = -(-planes // 8) * 8

    def shift(x, k):
        return lax.ppermute(x, "grid", [(i, (i + k) % slices) for i in range(slices)])

    def shift_diagonal(x, k):
        pairs = [
            (i * slices + j, (i ^ 1) * slices + (j + k) % slices) for i in range(groups) for j in range(slices)
        ]
        return lax.ppermute(x, ("band", "grid"), pairs)

    def other_core(x):
        return lax.ppermute(x, "band", [(i, i ^ 1) for i in range(groups)])

    piece = jax.ShapeDtypeStruct((each, rows, LANES), F32)
    packed = pl.pallas_call(
        functools.partial(pack_kernel, slices),
        out_shape=[piece] * slices,
        in_specs=in_vmem(1),
        out_specs=in_vmem(slices),
        scratch_shapes=[pltpu.VMEM((block * rows, LANES), F32)],
        compiler_params=params(8),
        name="pack",
    )(block_coeffs)
    coeffs = [packed[0]] + [shift(packed[k], k) for k in range(1, slices)]

    z_high, z_low = halves(np.concatenate([PROJECT.T, PROJECT.T], axis=1))
    project_tables = sheet(
        (NG + NP, 3 * LANES), (0, 0, z_high), (0, LANES, z_low), (NG, 0, left_table(PROJECT))
    )
    projected = pl.pallas_call(
        functools.partial(project_kernel, ways),
        out_shape=jax.ShapeDtypeStruct((planes, NP * NP), F32),
        in_specs=in_vmem(2) + [pl.BlockSpec(memory_space=pl.ANY)],
        out_specs=pl.BlockSpec(memory_space=pltpu.VMEM),
        scratch_shapes=[pltpu.VMEM((NG * planes, LANES), F32), pltpu.VMEM((NP * planes, LANES), F32)],
        compiler_params=params(12),
        name="project",
    )(potential, project_tables, packed[0])
    projected, coeffs = lax.optimization_barrier((projected, coeffs))
    own_pieces = [projected, other_core(projected)] if ways > 1 else [projected]

    eye = np.eye(QUAD)
    z_high, z_low = halves(np.kron(eye, TABLE.T))
    back_high, back_low = halves(np.kron(eye, TABLE))
    slots = np.zeros((NP, slices, ways, slot))
    slots[..., :planes] = PROJECT.reshape(NP, slices, ways, planes)
    tables = sheet(
        (ROW_PROJECT + slices * NP, 2 * LANES),
        (ROW_SYN, 0, left_table(TABLE[:, KX_ORDER])),
        (ROW_SYN, LANES, left_table(TABLE[Y_ORDER])),
        (ROW_ANA, 0, summed_table(TABLE[Y_ORDER].T)),
        (ROW_ANA, 2 * NP, summed_table(TABLE[:, KX_ORDER].T)),
        (ROW_Z_SYN, 0, np.concatenate([z_high, z_low, z_high], axis=0)),
        (ROW_Z_ANA, 0, np.concatenate([back_high, back_low], axis=1)),
        *[(ROW_PROJECT + k * NP, 0, left_table(slots[:, k].reshape(NP, -1))) for k in range(slices)],
    )
    cube = jax.ShapeDtypeStruct((KEEP, KEEP, LANES), F32)
    c_all, field, tables, projection, owners = pl.pallas_call(
        functools.partial(synthesis_kernel, slices, ways),
        out_shape=[
            cube,
            jax.ShapeDtypeStruct((NP * NP, 2 * LANES), F32),
            jax.ShapeDtypeStruct(tables.shape, tables.dtype),
            jax.ShapeDtypeStruct((NP, NP * NP), F32),
            jax.ShapeDtypeStruct((1, steps), jnp.int32),
        ],
        in_specs=in_vmem(slices + ways + 2),
        out_specs=in_vmem(5),
        scratch_shapes=[
            pltpu.VMEM((KEEP * KEEP, 2 * LANES), F32),
            pltpu.VMEM((2, KEEP * NP, LANES), F32),
            pltpu.VMEM((ways * slot, NP * NP), F32),
        ],
        compiler_params=params(20),
        cost_estimate=pl.CostEstimate(flops=1, bytes_accessed=1, transcendentals=0),
        name="synthesis",
    )(*coeffs, *own_pieces, tables, owners.reshape(1, steps))

    pieces = []
    for k in range(1, slices):
        if ways == 1:
            pieces.append(shift(projected, k))
        else:
            came, c_all, field = lax.optimization_barrier((shift_diagonal(projected, k), c_all, field))
            pieces += [other_core(came), came]

    *filtered_pieces, spread = pl.pallas_call(
        functools.partial(filter_kernel, slices, ways),
        out_shape=[piece] * slices
        + [jax.ShapeDtypeStruct((groups * slices, each * rows // groups, LANES), F32)],
        in_specs=in_vmem(3 + (slices - 1) * ways) + [pl.BlockSpec(memory_space=pltpu.SMEM)] * 2 + in_vmem(1),
        out_specs=in_vmem(slices + 1),
        scratch_shapes=[
            pltpu.VMEM((ways * slot, NP * NP), F32),
            pltpu.VMEM((NP if slices > 2 else 8, NP * NP), F32),
            pltpu.VMEM((NP * NP // 2, LANES), F32),
            pltpu.VMEM((KEEP, KEEP, LANES), F32),
            pltpu.VMEM((KEEP * KEEP, 2 * LANES), F32),
            pltpu.VMEM((2, KEEP * NP, LANES), F32),
            pltpu.VMEM((2, KEEP * NP, LANES), F32),
            pltpu.VMEM((each, KEEP * KEEP // LOW, LANES), F32),
        ],
        compiler_params=params(28),
        name="chebyshev",
    )(c_all, field, projection, *pieces, lower_edge, upper_edge, tables)
    arrived = [filtered_pieces[0]] + [shift(filtered_pieces[k], k) for k in range(1, slices)]
    filtered = pl.pallas_call(
        functools.partial(unpack_kernel, slices),
        out_shape=jax.ShapeDtypeStruct((block, cols), F32),
        in_specs=in_vmem(slices),
        out_specs=pl.BlockSpec(memory_space=pltpu.VMEM),
        scratch_shapes=[pltpu.VMEM((block * rows, LANES), F32)],
        compiler_params=params(8),
        cost_estimate=pl.CostEstimate(flops=1, bytes_accessed=1, transcendentals=0),
        name="unpack",
    )(*arrived)

    flat = jnp.transpose(rotation, (1, 0, 2)).reshape(rotation.shape[1], steps * block)
    high = lax.reduce_precision(flat, exponent_bits=8, mantissa_bits=7)
    table = jnp.concatenate([high, flat - high, high], axis=1).astype(BF16)

    came = lax.all_to_all(spread, ("band", "grid"), split_axis=0, concat_axis=0, tiled=True)
    came, table = lax.optimization_barrier((came, table))
    width = cols // groups
    mine = pl.pallas_call(
        select_kernel,
        out_shape=[jax.ShapeDtypeStruct((steps * block // 2, width), F32)] * 2,
        in_specs=[pl.BlockSpec(memory_space=pltpu.SMEM), pl.BlockSpec(memory_space=pltpu.VMEM)],
        out_specs=in_vmem(2),
        compiler_params=params(8),
        name="select",
    )(owners, came.reshape(-1, LANES))

    chips = groups // 2
    ring = list(range(0, chips, 2)) + list(range(1, chips, 2))[::-1]

    def pass_on(x, step):
        pairs = [
            (2 * ring[p] + c, 2 * ring[(p + step) % chips] + c) for p in range(chips) for c in range(2)
        ]
        return lax.ppermute(x, "band", pairs)

    rotated_shape = jax.ShapeDtypeStruct((rotation.shape[1], cols), F32)

    def rotate(moves, before, keep=0):
        arrays, plan = [], []
        for offset, flip, parts in moves:
            if isinstance(parts, tuple):
                arrays += parts[:1] if parts[1] == 0 else []
                plan.append((offset, flip, -1 - parts[1]))
            else:
                arrays += parts
                plan.append((offset, flip, len(parts)))
        depth = min(3, len(moves))
        kept = [jax.ShapeDtypeStruct((keep, steps * block, width), F32)] if keep else []
        return pl.pallas_call(
            functools.partial(rotate_kernel, tuple(plan), chips, bool(before), keep),
            out_shape=[jax.ShapeDtypeStruct((rotation.shape[1], cols), F32)] + kept,
            in_specs=in_vmem(1 + len(arrays)) + [pl.BlockSpec(memory_space=pl.ANY)] * len(before),
            out_specs=[pl.BlockSpec(memory_space=pl.ANY)] + in_vmem(len(kept)),
            scratch_shapes=[
                pltpu.VMEM((depth, rotation.shape[1], width), F32),
                pltpu.SemaphoreType.DMA((depth,)),
            ],
            input_output_aliases={len(arrays) + 1: 0} if before else {},
            compiler_params=params(16),
            cost_estimate=pl.CostEstimate(flops=1_000_000_000, bytes_accessed=4_000_000, transcendentals=0),
            name="rotate",
        )(table, *arrays, *before)

    half = chips // 2
    right, left = list(mine), list(mine)
    own = [(0, 0, list(mine))]
    for k in range(1, half):
        right, left = [pass_on(x, 1) for x in right], [pass_on(x, -1) for x in left]
        if k == half - 2:
            filtered, left[1] = lax.optimization_barrier((filtered, left[1]))
        if k == half - 1:
            early, kept = rotate(own, [], len(own))
            right, left, early, kept = lax.optimization_barrier((right, left, early, kept))
            together = other_core(kept)
            ready = [(offset, 1, (together, i)) for i, (offset, _, _) in enumerate(own)]
            own = []
        own += [(-k, 0, right), (k, 0, left)]
    last = [pass_on(right[0], 1), pass_on(left[1], -1)]
    early, kept = rotate(own + ready, [early], len(own))
    last, early, kept = lax.optimization_barrier((last, early, kept))
    together = other_core(kept)
    later = [(offset, 1, (together, i)) for i, (offset, _, _) in enumerate(own)]
    rotated, = rotate([(half, 0, last)], [early])
    rotated, = rotate(later + [(half, 1, [other_core(x) for x in last])], [rotated])
    return (filtered, rotated)


def solution(mesh):
    return jax.shard_map(
        body,
        mesh=mesh,
        in_specs=(P("band", "grid"), P("grid", None), P(), P(), P(None, "band", None), P()),
        out_specs=(P("band", "grid"), P("band", "grid")),
        check_vma=False,
    )
```

```python
import functools

import jax
import jax.numpy as jnp
import ml_dtypes
import numpy as np
from jax import lax
from jax.experimental import pallas as pl
from jax.experimental.pallas import tpu as pltpu
from jax.sharding import PartitionSpec as P

NG = 96
KEEP = 32
EDGE_ENERGY = 1.3
NP = 64
LOW = 4
LANES = LOW * KEEP
QUAD = 4
GROUP = 16
MIB = 1024 * 1024

F32 = jnp.float32
BF16 = jnp.bfloat16


def cas(angle):
    return np.cos(angle) + np.sin(angle)


SIGNED = np.where(np.arange(KEEP) < KEEP // 2, np.arange(KEEP), np.arange(KEEP) - KEEP).astype(np.float64)
POINTS = 2.0 * np.pi * (np.arange(NP) + 0.5) / NP


def product_basis(points):
    return np.concatenate(
        [np.cos(points[:, None] * np.arange(KEEP)), np.sin(points[:, None] * np.arange(1, KEEP + 1))], axis=1
    )


PROJECT = np.linalg.solve(product_basis(POINTS).T, product_basis(2.0 * np.pi * np.arange(NG) / NG).T)
TABLE = cas(POINTS[:, None] * SIGNED[None, :]) / np.sqrt(NG)
Y_ORDER = np.arange(NP).reshape(NP // 2, 2).T.reshape(-1)
KX_ORDER = np.arange(KEEP).reshape(KEEP // LOW, LOW).T.reshape(-1)


ROW_SYN, ROW_ANA = 0, NP
ROW_Z_SYN = ROW_ANA + 2 * KEEP
ROW_Z_ANA = ROW_Z_SYN + 3 * LANES
ROW_PROJECT = ROW_Z_ANA + 2 * LANES


def halves(table):
    high = table.astype(np.float32).astype(ml_dtypes.bfloat16)
    low = (table - high.astype(np.float64)).astype(np.float32).astype(ml_dtypes.bfloat16)
    return high, low


def left_table(table):
    high, low = halves(table)
    return np.concatenate([high, low, high], axis=1)


def summed_table(table):
    high, low = halves(table)
    return np.concatenate(
        [np.concatenate([high, high], axis=1), np.concatenate([low, np.zeros_like(low)], axis=1)], axis=0
    )


def split(x):
    high = x.astype(BF16)
    return high, (x - high.astype(F32)).astype(BF16)


def stack(x):
    high, low = split(x)
    return jnp.concatenate([high, high, low], axis=0)


def times(table, parts):
    res = mm(table, stack(jnp.concatenate(parts, axis=1)))
    width = parts[0].shape[1]
    return [res[:, i * width:(i + 1) * width] for i in range(len(parts))]


def times_summed(table, parts):
    res = mm(table, jnp.concatenate(split(jnp.concatenate(parts, axis=1)), axis=0))
    half, width = res.shape[0] // 2, parts[0].shape[1]
    res = res[:half] + res[half:]
    return [res[:, i * width:(i + 1) * width] for i in range(len(parts))]


def mm(a, b):
    return jnp.dot(a, b, preferred_element_type=F32)


def sheet(shape, *parts):
    whole = np.zeros(shape, ml_dtypes.bfloat16)
    for row, lane, part in parts:
        whole[row:row + part.shape[0], lane:lane + part.shape[1]] = part
    return jnp.asarray(whole)


def lane_transpose(parts):
    lane = lax.broadcasted_iota(jnp.int32, (1, LANES), 1)
    second = (lane // 64) == 1
    odd = (lane // 32) % 2 == 1
    a, b, c, d = parts
    p0 = jnp.where(second, pltpu.roll(c, 64, 1), a)
    p2 = jnp.where(second, c, pltpu.roll(a, 64, 1))
    p1 = jnp.where(second, pltpu.roll(d, 64, 1), b)
    p3 = jnp.where(second, d, pltpu.roll(b, 64, 1))
    r0 = jnp.where(odd, pltpu.roll(p1, 32, 1), p0)
    r1 = jnp.where(odd, p1, pltpu.roll(p0, 96, 1))
    r2 = jnp.where(odd, pltpu.roll(p3, 32, 1), p2)
    r3 = jnp.where(odd, p3, pltpu.roll(p2, 96, 1))
    return [r0, r1, r2, r3]


def pack_kernel(slices, c_ref, *rest):
    outs, scratch = rest[:slices], rest[slices]
    rows = scratch.shape[0] // 8
    each = 8 // slices
    g = lax.axis_index("grid")
    for r in range(rows):
        scratch[pl.ds(r, 8, stride=rows), :] = c_ref[:, r * LANES:(r + 1) * LANES]
    for k in range(slices):
        dest = lax.rem(g + k, slices)
        start = pl.multiple_of(dest * (each * rows), each * rows)
        outs[k][...] = scratch[pl.ds(start, each * rows), :].reshape(each, rows, LANES)


def unpack_kernel(slices, *refs):
    ins, (out, scratch) = refs[:slices], refs[slices:]
    rows = scratch.shape[0] // 8
    each = 8 // slices
    g = lax.axis_index("grid")
    for k in range(slices):
        source = lax.rem(g + slices - k, slices)
        start = pl.multiple_of(source * (each * rows), each * rows)
        scratch[pl.ds(start, each * rows), :] = ins[k][...].reshape(each * rows, LANES)
    for r in range(rows):
        out[:, r * LANES:(r + 1) * LANES] = scratch[pl.ds(r, 8, stride=rows), :]


def project_kernel(ways, v_ref, tables, after, out_ref, first, second):
    planes = out_ref.shape[0]
    start = 0
    if ways > 1:
        start = pl.multiple_of(lax.rem(lax.axis_index("band"), ways) * planes, planes)
    z_high, z_low = tables[:NG, :LANES], tables[:NG, LANES:2 * LANES]
    group = 16
    for y0 in range(0, NG, group):
        x = jnp.concatenate(
            [v_ref[pl.ds(start, planes), (y0 + i) * NG:(y0 + i + 1) * NG] for i in range(group)], axis=0
        )
        high, low = split(x)
        first[y0 * planes:(y0 + group) * planes, :] = mm(high, z_high) + mm(high, z_low) + mm(low, z_high)
    y_table = tables[NG:NG + NP, :3 * NG]
    for p in range(0, planes, 2):
        x = jnp.concatenate([first[pl.ds(p + i, NG, stride=planes), :] for i in range(2)], axis=1)
        res, = times(y_table, [x])
        for i in range(2):
            second[pl.ds(p + i, NP, stride=planes), :] = res[:, i * LANES:(i + 1) * LANES]
    left = lax.broadcasted_iota(jnp.int32, (1, LANES), 1) < NP
    for j in range(NP // 2):
        even = second[2 * j * planes:(2 * j + 1) * planes, :]
        odd = second[(2 * j + 1) * planes:(2 * j + 2) * planes, :]
        out_ref[:, j * LANES:(j + 1) * LANES] = jnp.where(left, even, odd)


def synthesis_kernel(slices, ways, *refs):
    coeffs, pieces, (tables, who) = refs[:slices], refs[slices:slices + ways], refs[slices + ways:slices + ways + 2]
    c_all, field, tables_out, projection, who_out, z_first, x1, planes_now = refs[slices + ways + 2:]
    tables_out[...] = tables[...]
    who_out[...] = who[...]
    g = lax.axis_index("grid")
    each, rows, _ = coeffs[0].shape
    ky_local = KEEP // slices
    kx_high = KEEP // LOW
    for k in range(slices):
        source = lax.rem(g + slices - k, slices)
        parts = [coeffs[k][b] if b < each else jnp.zeros((rows, LANES), F32) for b in range(QUAD)]
        for low, part in enumerate(lane_transpose(parts)):
            c_all[pl.ds(source * ky_local, ky_local), low * kx_high:(low + 1) * kx_high, :] = part.reshape(
                ky_local, kx_high, LANES
            )
    project_x(pieces, g, tables, planes_now, lambda lanes, value: put_lanes(projection, lanes, value))
    synthesize(c_all, tables, z_first, x1, lambda x, values: put(field, x * NP, jnp.concatenate(values, axis=0)))


def put_lanes(ref, lanes, value):
    ref[:, lanes] = value


def project_x(pieces, source, tables, planes_now, give):
    ways = len(pieces)
    planes = pieces[0].shape[0]
    slot = planes_now.shape[0] // ways
    core = lax.rem(lax.axis_index("band"), ways)
    if slot != planes:
        planes_now[...] = jnp.zeros_like(planes_now)
    for w in range(ways):
        start = pl.multiple_of(lax.rem(core + w, ways) * slot, slot)
        planes_now[pl.ds(start, planes), :] = pieces[w][...]
    row = pl.multiple_of(ROW_PROJECT + source * NP, NP)
    table = tables[pl.ds(row, NP), :][:, :3 * ways * slot]
    width = 512
    for lane in range(0, NP * NP, width):
        give(slice(lane, lane + width), mm(table, stack(planes_now[:, lane:lane + width])))


def put(ref, row, value):
    ref[row:row + value.shape[0], :] = value


def put_wide(ref, row, value):
    for h in range(2):
        ref[h, row:row + value.shape[0], :] = value[:, h * LANES:(h + 1) * LANES]


def wide(ref, start, size, stride):
    return jnp.concatenate([ref[h, pl.ds(start, size, stride=stride), :] for h in range(2)], axis=1)


def synthesize(u_all, tables, z_first, x1, give):
    z_syn = tables[ROW_Z_SYN:ROW_Z_SYN + 3 * LANES, :2 * LANES]
    group = 16
    for ky in range(0, KEEP, group):
        high, low = split(u_all[ky:ky + group].reshape(group * KEEP, LANES))
        put(z_first, ky * KEEP, mm(jnp.concatenate([high, high, low], axis=1), z_syn))
    xs = tables[ROW_SYN:ROW_SYN + NP, :3 * KEEP]
    for ky in range(0, KEEP, GROUP):
        parts = [z_first[(ky + i) * KEEP:(ky + i + 1) * KEEP, :] for i in range(GROUP)]
        for i, res in enumerate(times(xs, parts)):
            put_wide(x1, (ky + i) * NP, res)
    ys = tables[ROW_SYN:ROW_SYN + NP, LANES:LANES + 3 * KEEP]
    for x in range(0, NP, GROUP):
        give(x, times(ys, [wide(x1, x + i, KEEP, NP) for i in range(GROUP)]))


def filter_kernel(slices, ways, *refs):
    c_all, field, projection = refs[:3]
    pieces = refs[3:3 + (slices - 1) * ways]
    refs = refs[3 + (slices - 1) * ways:]
    lower, upper, tables = refs[:3]
    outs, spread = refs[3:3 + slices], refs[3 + slices]
    planes_now, total, vx, u_all, z_first, x1, y2, packed = refs[4 + slices:]
    g = lax.axis_index("grid")
    each, rows, _ = outs[0].shape
    kx_high = KEEP // LOW

    def add(lanes, value):
        total[:, lanes] += value

    def finish_projection(lanes, value):
        value = value + (projection if slices == 2 else total)[:, lanes]
        for j in range(value.shape[1] // LANES):
            put(vx, (lanes.start // LANES + j) * NP, value[:, j * LANES:(j + 1) * LANES])

    if slices > 2:
        total[...] = projection[...]
    for k in range(1, slices):
        project_x(
            pieces[(k - 1) * ways:k * ways],
            lax.rem(g + slices - k, slices),
            tables,
            planes_now,
            finish_projection if k == slices - 1 else add,
        )
    left = lax.broadcasted_iota(jnp.int32, (1, LANES), 1) < NP

    low_edge = jnp.full((1, LANES), lower[0], F32)
    high_edge = jnp.full((1, LANES), upper[0], F32)
    center = (low_edge + high_edge) * 0.5
    half_width = (high_edge - low_edge) * 0.5

    row = lax.broadcasted_iota(jnp.int32, (KEEP, LANES), 0)
    lane = lax.broadcasted_iota(jnp.int32, (KEEP, LANES), 1)
    kx = row % kx_high * LOW + row // kx_high
    kz = lane % KEEP
    signed = [jnp.where(k < KEEP // 2, k, k - KEEP).astype(F32) for k in (kx, kz)]
    square = signed[0] * signed[0] + signed[1] * signed[1]

    z_ana = tables[ROW_Z_ANA:ROW_Z_ANA + 2 * LANES, :2 * LANES]
    ya = tables[ROW_ANA:ROW_ANA + 2 * KEEP, :2 * NP]
    xa = tables[ROW_ANA:ROW_ANA + 2 * KEEP, 2 * NP:4 * NP]

    def weigh(x, values):
        parts = []
        for i, value in enumerate(values):
            local = vx[pl.ds(x + i, NP // 2, stride=NP), :]
            turned = pltpu.roll(local, NP, 1)
            local = jnp.concatenate([jnp.where(left, local, turned), jnp.where(left, turned, local)], axis=0)
            parts.append(value * jnp.concatenate([local, local], axis=1))
        for i, res in enumerate(times_summed(ya, parts)):
            put_wide(y2, (x + i) * KEEP, res)

    def finish(u, scale, back):
        for ky in range(0, KEEP, GROUP):
            res = times_summed(xa, [wide(y2, ky + i, NP, KEEP) for i in range(GROUP)])
            put(z_first, ky * KEEP, jnp.concatenate(res, axis=0))
        group = 8
        for ky in range(0, KEEP, group):
            high, low = split(z_first[ky * KEEP:(ky + group) * KEEP, :])
            twice = mm(high, z_ana)
            res = twice[:, :LANES] + twice[:, LANES:] + mm(low, z_ana[:, :LANES])
            for i in range(group):
                kinetic = EDGE_ENERGY * ((square + SIGNED[ky + i] ** 2) * (1.0 / (KEEP // 2) ** 2))
                now = u[ky + i]
                out = scale * (kinetic * now + res[i * KEEP:(i + 1) * KEEP, :] - center * now)
                u_all[ky + i] = out - c_all[ky + i] if back else out

    for x in range(0, NP, GROUP):
        weigh(x, [field[(x + i) * NP:(x + i + 1) * NP, :] for i in range(GROUP)])
    finish(c_all, 1.0 / half_width, False)
    synthesize(u_all, tables, z_first, x1, weigh)
    finish(u_all, 2.0 / half_width, True)

    parts = [
        u_all[:, low * kx_high:(low + 1) * kx_high, :].reshape(KEEP * kx_high, LANES) for low in range(LOW)
    ]
    for b, part in enumerate(lane_transpose(parts)[:each]):
        packed[b] = part
    for k in range(slices):
        dest = lax.rem(g + k, slices)
        start = pl.multiple_of(dest * rows, rows)
        for b in range(each):
            outs[k][b] = packed[b, pl.ds(start, rows), :]
    run = spread.shape[1] // each
    groups = rows // run
    for dest in range(groups * slices):
        start = (dest % slices) * rows + (dest // slices) * run
        for b in range(each):
            spread[dest, b * run:(b + 1) * run, :] = packed[b, start:start + run, :]


def select_kernel(owners, came, *outs):
    steps = owners.shape[1]
    run = outs[0].shape[1] // LANES
    each = steps // len(outs)
    block = outs[0].shape[0] // each
    for s in range(steps):
        out, row = outs[s // each], s % each * block
        for r in range(run):
            start = owners[0, s] * (block * run) + r
            out[row:row + block, r * LANES:(r + 1) * LANES] = came[pl.ds(start, block, stride=run), :]


def rotate_kernel(moves, chips, continued, keep, table, *refs):
    refs = list(refs)
    results, sems = refs[-2:]
    together = None
    pieces = []
    for _, _, parts in moves:
        if parts < 0:
            together = refs.pop(0) if together is None else together
            pieces.append([together.at[-1 - parts]])
        else:
            pieces.append([refs.pop(0) for _ in range(parts)])
    if continued:
        refs.pop(0)
    out, kept = refs[0], refs[1] if keep else None
    band = lax.axis_index("band")
    chip, core = band // 2, lax.rem(band, 2)
    position = jnp.where(lax.rem(chip, 2) == 0, chip // 2, chips - 1 - chip // 2)
    slots, _, width = results.shape
    left = table[...]
    stores = []
    for j, ((offset, flip, _), parts) in enumerate(zip(moves, pieces)):
        block = jnp.concatenate([part[...] for part in parts], axis=0)
        if j < keep:
            kept[j] = block
        res = mm(left, stack(block))
        if j >= slots:
            stores[j - slots].wait()
        results[j % slots] = res
        place = lax.rem(position + (chips + offset), chips)
        owner = jnp.where(place < chips // 2, 2 * place, 2 * (chips - 1 - place) + 1)
        start = pl.multiple_of((2 * owner + (core if flip == 0 else 1 - core)) * width, width)
        store = pltpu.make_async_copy(results.at[j % slots], out.at[:, pl.ds(start, width)], sems.at[j % slots])
        store.start()
        stores.append(store)
    for store in stores[-slots:]:
        store.wait()


def params(mib):
    return pltpu.CompilerParams(vmem_limit_bytes=mib * MIB)


def in_vmem(count):
    return [pl.BlockSpec(memory_space=pltpu.VMEM)] * count


def body(block_coeffs, potential, lower_edge, upper_edge, rotation, owners):
    slices = lax.axis_size("grid")
    groups = lax.axis_size("band")
    block, cols = block_coeffs.shape
    rows = cols // LANES
    each = block // slices
    steps = rotation.shape[0]
    ways = 2 if potential.shape[0] % 16 == 0 else 1
    planes = potential.shape[0] // ways
    slot = -(-planes // 8) * 8

    def shift(x, k):
        return lax.ppermute(x, "grid", [(i, (i + k) % slices) for i in range(slices)])

    def shift_diagonal(x, k):
        pairs = [
            (i * slices + j, (i ^ 1) * slices + (j + k) % slices) for i in range(groups) for j in range(slices)
        ]
        return lax.ppermute(x, ("band", "grid"), pairs)

    def other_core(x):
        return lax.ppermute(x, "band", [(i, i ^ 1) for i in range(groups)])

    piece = jax.ShapeDtypeStruct((each, rows, LANES), F32)
    packed = pl.pallas_call(
        functools.partial(pack_kernel, slices),
        out_shape=[piece] * slices,
        in_specs=in_vmem(1),
        out_specs=in_vmem(slices),
        scratch_shapes=[pltpu.VMEM((block * rows, LANES), F32)],
        compiler_params=params(8),
        name="pack",
    )(block_coeffs)
    coeffs = [packed[0]] + [shift(packed[k], k) for k in range(1, slices)]

    z_high, z_low = halves(np.concatenate([PROJECT.T, PROJECT.T], axis=1))
    project_tables = sheet(
        (NG + NP, 3 * LANES), (0, 0, z_high), (0, LANES, z_low), (NG, 0, left_table(PROJECT))
    )
    projected = pl.pallas_call(
        functools.partial(project_kernel, ways),
        out_shape=jax.ShapeDtypeStruct((planes, NP * NP), F32),
        in_specs=in_vmem(2) + [pl.BlockSpec(memory_space=pl.ANY)],
        out_specs=pl.BlockSpec(memory_space=pltpu.VMEM),
        scratch_shapes=[pltpu.VMEM((NG * planes, LANES), F32), pltpu.VMEM((NP * planes, LANES), F32)],
        compiler_params=params(12),
        name="project",
    )(potential, project_tables, packed[0])
    projected, coeffs = lax.optimization_barrier((projected, coeffs))
    own_pieces = [projected, other_core(projected)] if ways > 1 else [projected]

    eye = np.eye(QUAD)
    z_high, z_low = halves(np.kron(eye, TABLE.T))
    back_high, back_low = halves(np.kron(eye, TABLE))
    slots = np.zeros((NP, slices, ways, slot))
    slots[..., :planes] = PROJECT.reshape(NP, slices, ways, planes)
    tables = sheet(
        (ROW_PROJECT + slices * NP, 2 * LANES),
        (ROW_SYN, 0, left_table(TABLE[:, KX_ORDER])),
        (ROW_SYN, LANES, left_table(TABLE[Y_ORDER])),
        (ROW_ANA, 0, summed_table(TABLE[Y_ORDER].T)),
        (ROW_ANA, 2 * NP, summed_table(TABLE[:, KX_ORDER].T)),
        (ROW_Z_SYN, 0, np.concatenate([z_high, z_low, z_high], axis=0)),
        (ROW_Z_ANA, 0, np.concatenate([back_high, back_low], axis=1)),
        *[(ROW_PROJECT + k * NP, 0, left_table(slots[:, k].reshape(NP, -1))) for k in range(slices)],
    )
    cube = jax.ShapeDtypeStruct((KEEP, KEEP, LANES), F32)
    c_all, field, tables, projection, owners = pl.pallas_call(
        functools.partial(synthesis_kernel, slices, ways),
        out_shape=[
            cube,
            jax.ShapeDtypeStruct((NP * NP, 2 * LANES), F32),
            jax.ShapeDtypeStruct(tables.shape, tables.dtype),
            jax.ShapeDtypeStruct((NP, NP * NP), F32),
            jax.ShapeDtypeStruct((1, steps), jnp.int32),
        ],
        in_specs=in_vmem(slices + ways + 2),
        out_specs=in_vmem(5),
        scratch_shapes=[
            pltpu.VMEM((KEEP * KEEP, 2 * LANES), F32),
            pltpu.VMEM((2, KEEP * NP, LANES), F32),
            pltpu.VMEM((ways * slot, NP * NP), F32),
        ],
        compiler_params=params(20),
        cost_estimate=pl.CostEstimate(flops=1, bytes_accessed=1, transcendentals=0),
        name="synthesis",
    )(*coeffs, *own_pieces, tables, owners.reshape(1, steps))

    pieces = []
    for k in range(1, slices):
        if ways == 1:
            pieces.append(shift(projected, k))
        else:
            came, c_all, field = lax.optimization_barrier((shift_diagonal(projected, k), c_all, field))
            pieces += [other_core(came), came]

    *filtered_pieces, spread = pl.pallas_call(
        functools.partial(filter_kernel, slices, ways),
        out_shape=[piece] * slices
        + [jax.ShapeDtypeStruct((groups * slices, each * rows // groups, LANES), F32)],
        in_specs=in_vmem(3 + (slices - 1) * ways) + [pl.BlockSpec(memory_space=pltpu.SMEM)] * 2 + in_vmem(1),
        out_specs=in_vmem(slices + 1),
        scratch_shapes=[
            pltpu.VMEM((ways * slot, NP * NP), F32),
            pltpu.VMEM((NP if slices > 2 else 8, NP * NP), F32),
            pltpu.VMEM((NP * NP // 2, LANES), F32),
            pltpu.VMEM((KEEP, KEEP, LANES), F32),
            pltpu.VMEM((KEEP * KEEP, 2 * LANES), F32),
            pltpu.VMEM((2, KEEP * NP, LANES), F32),
            pltpu.VMEM((2, KEEP * NP, LANES), F32),
            pltpu.VMEM((each, KEEP * KEEP // LOW, LANES), F32),
        ],
        compiler_params=params(28),
        name="chebyshev",
    )(c_all, field, projection, *pieces, lower_edge, upper_edge, tables)
    arrived = [filtered_pieces[0]] + [shift(filtered_pieces[k], k) for k in range(1, slices)]
    filtered = pl.pallas_call(
        functools.partial(unpack_kernel, slices),
        out_shape=jax.ShapeDtypeStruct((block, cols), F32),
        in_specs=in_vmem(slices),
        out_specs=pl.BlockSpec(memory_space=pltpu.VMEM),
        scratch_shapes=[pltpu.VMEM((block * rows, LANES), F32)],
        compiler_params=params(8),
        cost_estimate=pl.CostEstimate(flops=1, bytes_accessed=1, transcendentals=0),
        name="unpack",
    )(*arrived)

    flat = jnp.transpose(rotation, (1, 0, 2)).reshape(rotation.shape[1], steps * block)
    high = lax.reduce_precision(flat, exponent_bits=8, mantissa_bits=7)
    table = jnp.concatenate([high, flat - high, high], axis=1).astype(BF16)

    came = lax.all_to_all(spread, ("band", "grid"), split_axis=0, concat_axis=0, tiled=True)
    came, table = lax.optimization_barrier((came, table))
    width = cols // groups
    mine = pl.pallas_call(
        select_kernel,
        out_shape=[jax.ShapeDtypeStruct((steps * block // 2, width), F32)] * 2,
        in_specs=[pl.BlockSpec(memory_space=pltpu.SMEM), pl.BlockSpec(memory_space=pltpu.VMEM)],
        out_specs=in_vmem(2),
        compiler_params=params(8),
        name="select",
    )(owners, came.reshape(-1, LANES))

    chips = groups // 2
    ring = list(range(0, chips, 2)) + list(range(1, chips, 2))[::-1]

    def pass_on(x, step):
        pairs = [
            (2 * ring[p] + c, 2 * ring[(p + step) % chips] + c) for p in range(chips) for c in range(2)
        ]
        return lax.ppermute(x, "band", pairs)

    rotated_shape = jax.ShapeDtypeStruct((rotation.shape[1], cols), F32)

    def rotate(moves, before, keep=0):
        arrays, plan = [], []
        for offset, flip, parts in moves:
            if isinstance(parts, tuple):
                arrays += [] if any(x is parts[0] for x in arrays) else parts[:1]
                plan.append((offset, flip, -1 - parts[1]))
            else:
                arrays += parts
                plan.append((offset, flip, len(parts)))
        depth = min(3, len(moves))
        kept = [jax.ShapeDtypeStruct((keep, steps * block, width), F32)] if keep else []
        return pl.pallas_call(
            functools.partial(rotate_kernel, tuple(plan), chips, bool(before), keep),
            out_shape=[jax.ShapeDtypeStruct((rotation.shape[1], cols), F32)] + kept,
            in_specs=in_vmem(1 + len(arrays)) + [pl.BlockSpec(memory_space=pl.ANY)] * len(before),
            out_specs=[pl.BlockSpec(memory_space=pl.ANY)] + in_vmem(len(kept)),
            scratch_shapes=[
                pltpu.VMEM((depth, rotation.shape[1], width), F32),
                pltpu.SemaphoreType.DMA((depth,)),
            ],
            input_output_aliases={len(arrays) + 1: 0} if before else {},
            compiler_params=params(16),
            cost_estimate=pl.CostEstimate(flops=1_000_000_000, bytes_accessed=4_000_000, transcendentals=0),
            name="rotate",
        )(table, *arrays, *before)

    half = chips // 2
    right, left = list(mine), list(mine)
    own = [(0, 0, list(mine))]
    for k in range(1, half):
        right, left = [pass_on(x, 1) for x in right], [pass_on(x, -1) for x in left]
        if k == half - 2:
            filtered, left[1] = lax.optimization_barrier((filtered, left[1]))
        if k == half - 1:
            early, kept = rotate(own, [], len(own))
            right, left, early, kept = lax.optimization_barrier((right, left, early, kept))
            together = other_core(kept)
            ready = [(offset, 1, (together, i)) for i, (offset, _, _) in enumerate(own)]
            own = []
        own += [(-k, 0, right), (k, 0, left)]
    last = [pass_on(right[0], 1), pass_on(left[1], -1)]
    early, kept = rotate(own + ready[:-2], [early], len(own))
    last, early, kept = lax.optimization_barrier((last, early, kept))
    together = other_core(kept)
    later = [(offset, 1, (together, i)) for i, (offset, _, _) in enumerate(own)]
    rotated, = rotate([(half, 0, last)] + ready[-2:], [early])
    rotated, = rotate(later + [(half, 1, [other_core(x) for x in last])], [rotated])
    return (filtered, rotated)


def solution(mesh):
    return jax.shard_map(
        body,
        mesh=mesh,
        in_specs=(P("band", "grid"), P("grid", None), P(), P(), P(None, "band", None), P()),
        out_specs=(P("band", "grid"), P("band", "grid")),
        check_vma=False,
    )
```
